256 devices in a mesh: row: 16 (over z_lo, y, core), col: 16 (over z_hi, x).
Axes of the slice: x: 4, y: 4, z: 8 (z_hi: 4, z_lo: 2; z = z_hi * 2 + z_lo), core: 2. Of those that a mesh axis runs over, the one named last changes fastest.
Arguments:
- inputs: bfloat16 [12288, 4096], P('col'), may hold values from -6 to 6
- cotangent: bfloat16 [12288, 4096], P('col', 'row'), may hold values from -6 to 6
- gate_weight: bfloat16 [4096, 14336], P('col', 'row'), may hold values from -0.09375 to 0.09375
- up_weight: bfloat16 [4096, 14336], P('col', 'row'), may hold values from -0.09375 to 0.09375
- proj_in: bfloat16 [14336, 128], P('row'), may hold values from -0.046875 to 0.046875
- proj_out: bfloat16 [4096, 128], P('row'), may hold values from -0.09375 to 0.09375
- inverse_fisher: bfloat16 [16384, 16384], P('row', 'col'), may hold values from -0.05 to 2.1
- stored: bfloat16 [16384, 16384], P('row', 'col'), may hold values from -0.014953613 to 0.014953613
Outputs:
- scores: float32 [192, 16384], P('col', 'row')
The draws below stay inside these ranges and needn't reach their ends.
All inputs are finite; a program needn't handle non-finite values.
Results may differ from the reference program's by a relative error of at most 0.005.
Values may be sent and summed in bfloat16 or wider, within the bound.
A program may use at most 256 MiB of HBM per device.

```python
import jax
import jax.numpy as jnp
from jax import lax

D = 4096
FF = 14336
KIN = 128
KOUT = 128
TOK_SEQ = 64
FEAT = 16384
SEQS = 192
TOKENS = 12288
NSTORE = 16384


def draw_inverse_fisher(key, part):
    key = jax.random.fold_in(key, 5)
    key_diag, key_rest = jax.random.split(key)
    diagonal = jnp.exp(jax.random.uniform(key_diag, (FEAT,), jnp.float32, jnp.log(0.5), jnp.log(2.0)))
    scatter_noise = 0.004 * jax.random.normal(key_rest, (FEAT, FEAT), jnp.float32)
    positions = jnp.arange(FEAT)
    return scatter_noise.at[positions, positions].add(diagonal).astype(jnp.bfloat16)


def steps_of(own_key, dims, cuts, least, high):
    loudness = 1.0
    for axis_at, blocks in cuts:
        heights = jax.random.uniform(jax.random.fold_in(jax.random.fold_in(own_key, 6), axis_at), (blocks,), jnp.float32, least / len(cuts), high / len(cuts))
        loudness = loudness * jnp.repeat(jnp.exp(heights), dims[axis_at] // blocks).reshape((-1,) + (1,) * (len(dims) - 1 - axis_at))
    return loudness


def scatter_about(stream_key, dims, scale, most, cuts=(), held_as=jnp.bfloat16):
    values = jax.random.normal(stream_key, dims, jnp.float32) * scale
    if len(cuts) > 0:
        values = steps_of(stream_key, dims, cuts, -0.22, 0.18) * values
    return jnp.clip(values, min=-most, max=most).astype(held_as)


def setup_inputs(seed: int = 0) -> dict:
    keys = jax.random.split(jax.random.key(seed), 9)
    inputs = scatter_about(keys[0], (TOKENS, D), 1.0, 6.0, ((0, 16),))
    cotangent = scatter_about(keys[1], (TOKENS, D), 1.0, 6.0, ((0, 16), (1, 16)))
    gate_weight = scatter_about(keys[2], (D, FF), D ** -0.5, 0.09375, ((0, 16), (1, 16)))
    up_weight = scatter_about(keys[3], (D, FF), D ** -0.5, 0.09375, ((0, 16), (1, 16)))
    proj_in = scatter_about(keys[4], (FF, KIN), FF ** -0.5, 0.046875, ((0, 16),))
    proj_out = scatter_about(keys[5], (D, KOUT), D ** -0.5, 0.09375, ((0, 16),))
    inverse_fisher = draw_inverse_fisher(jax.random.fold_in(keys[8], 71), 0)
    stored = scatter_about(keys[7], (NSTORE, FEAT), 0.0025, 0.014953613, ((0, 16), (1, 16)))
    return {"inputs": inputs, "cotangent": cotangent, "gate_weight": gate_weight, "up_weight": up_weight, "proj_in": proj_in, "proj_out": proj_out, "inverse_fisher": inverse_fisher, "stored": stored}


def reference(inputs, cotangent, gate_weight, up_weight, proj_in, proj_out, inverse_fisher, stored):
    gate_part = jnp.dot(inputs, gate_weight, preferred_element_type=jnp.float32)
    up_part = jnp.dot(inputs, up_weight, preferred_element_type=jnp.float32)
    hidden = (jax.nn.silu(gate_part) * up_part).astype(jnp.bfloat16)
    left_proj = jnp.dot(hidden, proj_in, preferred_element_type=jnp.float32)
    right_proj = jnp.dot(cotangent, proj_out, preferred_element_type=jnp.float32)
    seq_grads = jnp.einsum("sti,stj->sij", left_proj.reshape(SEQS, TOK_SEQ, KIN), right_proj.reshape(SEQS, TOK_SEQ, KOUT), precision=lax.Precision.HIGHEST)
    seq_grads = seq_grads.reshape(SEQS, FEAT).astype(jnp.bfloat16)
    precond = jnp.dot(seq_grads, inverse_fisher, preferred_element_type=jnp.float32).astype(jnp.bfloat16)
    return lax.dot_general(precond, stored, (((1,), (1,)), ((), ())), preferred_element_type=jnp.float32)
```

```python
import jax
import jax.numpy as jnp
from jax import lax
from jax.experimental import pallas as pl
from jax.experimental.pallas import tpu as pltpu
from jax.sharding import PartitionSpec as P

KIN = 128
KOUT = 128
TOK_SEQ = 64
N = 16
PAD = 16


def tail_kernel(
    left_ref, cot_ref, pout_ref, fisher_ref, stored_ref, out_ref,
    right_part, right_recv, right_own, right_all, left_recv,
    grads_own, grads_all, part, part_recv, prec_all, part2, part2_recv,
    send_sem, recv_sem, local_sem,
):
    row = lax.axis_index("row")
    col = lax.axis_index("col")
    tokens = cot_ref.shape[0]
    tok_blk = tokens // N
    seqs = tokens // TOK_SEQ

    def row_dev(d):
        return {"row": lax.rem(row + d, N), "col": col}

    def col_dev(d):
        return {"row": row, "col": lax.rem(col + d, N)}

    barrier = pltpu.get_barrier_semaphore()

    def greet(d, carry):
        pl.semaphore_signal(barrier, inc=1, device_id=row_dev(d))
        pl.semaphore_signal(barrier, inc=1, device_id=col_dev(d))
        return carry

    lax.fori_loop(1, N, greet, 0)

    right_part[...] = jnp.dot(cot_ref[...], pout_ref[...], preferred_element_type=jnp.float32)
    pl.semaphore_wait(barrier, 2 * (N - 1))

    def exchange(phase, src_of, dst_of, dev_of):
        def copy(d):
            return pltpu.make_async_remote_copy(
                src_ref=src_of(d), dst_ref=dst_of(d),
                send_sem=send_sem.at[phase, d], recv_sem=recv_sem.at[phase, d],
                device_id=dev_of(d),
            )

        def start(d, carry):
            copy(d).start()
            return carry

        def wait_recv(d, carry):
            copy(d).wait_recv()
            return carry

        def wait_send(d, carry):
            copy(d).wait_send()
            return carry

        lax.fori_loop(1, N, start, 0)
        return (
            lambda: lax.fori_loop(1, N, wait_recv, 0),
            lambda: lax.fori_loop(1, N, wait_send, 0),
        )

    def at_row(d):
        return lax.rem(row + d, N)

    def at_col(d):
        return lax.rem(col + d, N)

    right_in, right_sent = exchange(
        0, lambda d: right_part.at[pl.ds(at_row(d) * tok_blk, tok_blk)],
        lambda d: right_recv.at[d], row_dev)
    left_in, left_sent = exchange(
        1, lambda d: left_ref.at[pl.ds(at_row(d) * 8, 8)],
        lambda d: left_recv.at[d], row_dev)

    right_in()
    total = right_part[pl.ds(row * tok_blk, tok_blk), :]
    for d in range(1, N):
        total = total + right_recv[d]
    right_own[...] = total
    right_all[pl.ds(row * tok_blk, tok_blk), :] = total
    rall_in, rall_sent = exchange(
        2, lambda d: right_own,
        lambda d: right_all.at[pl.ds(row * tok_blk, tok_blk)], row_dev)

    left_in()
    left = left_ref[pl.ds(row * 8, 8), :]
    for d in range(1, N):
        left = left + left_recv[d]
    lane = lax.broadcasted_iota(jnp.int32, (PAD, tokens), 1)
    first = lax.broadcasted_iota(jnp.int32, (PAD, tokens), 0) * TOK_SEQ
    inside = (lane >= first) & (lane < first + TOK_SEQ)
    spread = jnp.concatenate(
        [jnp.where(inside, jnp.broadcast_to(left[i : i + 1, :], (PAD, tokens)), 0.0) for i in range(8)], axis=0)
    rall_in()
    grads = jnp.dot(spread, right_all[...], preferred_element_type=jnp.float32, precision=lax.Precision.HIGHEST)
    for i in range(8):
        piece = grads[i * PAD : (i + 1) * PAD, :].astype(jnp.bfloat16)
        grads_own[:, i * KOUT : (i + 1) * KOUT] = piece
        grads_all[pl.ds(pl.multiple_of(col * PAD, PAD), PAD), i * KOUT : (i + 1) * KOUT] = piece

    gall_in, gall_sent = exchange(
        3, lambda d: grads_own,
        lambda d: grads_all.at[pl.ds(col * PAD, PAD)], col_dev)
    gall_in()
    part[...] = jnp.dot(grads_all[...], fisher_ref[...], preferred_element_type=jnp.float32)
    part_in, part_sent = exchange(
        4, lambda d: part.at[pl.ds(at_row(d) * PAD, PAD)],
        lambda d: part_recv.at[d], row_dev)
    part_in()
    total = part[pl.ds(pl.multiple_of(row * PAD, PAD), PAD), :]
    for d in range(1, N):
        total = total + part_recv[d]
    own = total.astype(jnp.bfloat16)
    gall_sent()
    grads_own[...] = own
    prec_all[pl.ds(pl.multiple_of(row * PAD, PAD), PAD), :] = own
    pall_in, pall_sent = exchange(
        5, lambda d: grads_own,
        lambda d: prec_all.at[pl.ds(row * PAD, PAD)], row_dev)
    pall_in()
    part2[...] = lax.dot_general(
        prec_all[...], stored_ref[...], (((1,), (1,)), ((), ())), preferred_element_type=jnp.float32)
    part2_in, part2_sent = exchange(
        6, lambda d: part2.at[pl.ds(at_col(d) * PAD, PAD)],
        lambda d: part2_recv.at[d], col_dev)
    part2_in()
    total = part2[pl.ds(pl.multiple_of(col * PAD, PAD), PAD), :]
    for d in range(1, N):
        total = total + part2_recv[d]
    out_ref[...] = total[:seqs, :]
    for sent in (right_sent, left_sent, rall_sent, part_sent, pall_sent, part2_sent):
        sent()


def tail(left_t, cotangent, proj_out, fisher, stored):
    tokens = cotangent.shape[0]
    feats = fisher.shape[0]
    rows = N * PAD
    f32, bf16 = jnp.float32, jnp.bfloat16
    return pl.pallas_call(
        tail_kernel,
        out_shape=jax.ShapeDtypeStruct((tokens // TOK_SEQ, stored.shape[0]), f32),
        in_specs=[pl.BlockSpec(memory_space=pltpu.VMEM)] * 5,
        out_specs=pl.BlockSpec(memory_space=pltpu.VMEM),
        scratch_shapes=[
            pltpu.VMEM((tokens, KOUT), f32),
            pltpu.VMEM((N, tokens // N, KOUT), f32),
            pltpu.VMEM((tokens // N, KOUT), f32),
            pltpu.VMEM((tokens, KOUT), f32),
            pltpu.VMEM((N, 8, tokens), f32),
            pltpu.VMEM((PAD, feats), bf16),
            pltpu.VMEM((rows, feats), bf16),
            pltpu.VMEM((rows, feats), f32),
            pltpu.VMEM((N, PAD, feats), f32),
            pltpu.VMEM((rows, feats), bf16),
            pltpu.VMEM((rows, feats), f32),
            pltpu.VMEM((N, PAD, feats), f32),
            pltpu.SemaphoreType.DMA((7, N)),
            pltpu.SemaphoreType.DMA((7, N)),
            pltpu.SemaphoreType.DMA,
        ],
        compiler_params=pltpu.CompilerParams(
            collective_id=1, has_side_effects=True, vmem_limit_bytes=48 * 1024 * 1024),
        name="tail",
    )(left_t, cotangent, proj_out, fisher, stored)


def body(inputs, cotangent, gate_weight, up_weight, proj_in, proj_out, inverse_fisher, stored):
    gate_part = jnp.dot(
        inputs,
        lax.all_gather(gate_weight, "col", axis=0, tiled=True),
        preferred_element_type=jnp.float32,
    )
    up_part = jnp.dot(
        inputs,
        lax.all_gather(up_weight, "col", axis=0, tiled=True),
        preferred_element_type=jnp.float32,
    )
    hidden = (jax.nn.silu(gate_part) * up_part).astype(jnp.bfloat16)
    left_t = lax.dot_general(
        proj_in, hidden, (((0,), (1,)), ((), ())), preferred_element_type=jnp.float32)
    return tail(left_t, cotangent, proj_out, inverse_fisher, stored)


def solution(mesh):
    return jax.shard_map(
        body,
        mesh=mesh,
        in_specs=(
            P("col", None),
            P("col", "row"),
            P("col", "row"),
            P("col", "row"),
            P("row", None),
            P("row", None),
            P("row", "col"),
            P("row", "col"),
        ),
        out_specs=P("col", "row"),
        check_vma=False,
    )
```

```python
import jax
import jax.numpy as jnp
from jax import lax
from jax.experimental import pallas as pl
from jax.experimental.pallas import tpu as pltpu
from jax.sharding import PartitionSpec as P

KIN = 128
KOUT = 128
TOK_SEQ = 64
N = 16
PAD = 16


def place(zl, y, core, zh, x):
    return {"row": (zl * 4 + y) * 2 + core, "col": zh * 4 + x}


def ffn_kernel(
    x_hbm, gate_hbm, up_hbm, pin_hbm, left_ref,
    weights, acts, acc_gate, acc_up, pin,
    local_sem, z_send, z_recv, x_send, x_recv, sib_send, sib_recv, in_send, in_recv,
):
    row = lax.axis_index("row")
    col = lax.axis_index("col")
    core = lax.rem(row, 2)
    y = lax.rem(row // 2, 4)
    zl = row // 8
    x = lax.rem(col, 4)
    zh = col // 4
    kind = zh // 2
    native = core == kind
    beside = zh + 1 - 2 * lax.rem(zh, 2)
    across = 3 - zh
    across_beside = across + 1 - 2 * lax.rem(across, 2)
    next_to_across = lax.rem(zh, 2) == zl
    sources = (zh, beside, across, across_beside)
    right = lax.rem(x + 1, 4)
    left = lax.rem(x + 3, 4)
    far = lax.rem(x + 2, 4)
    up_y = lax.rem(y + 1, 4)
    down_y = lax.rem(y + 3, 4)
    far_y = lax.rem(y + 2, 4)
    depth = gate_hbm.shape[0]
    group = 4 * depth
    tokens = x_hbm.shape[0]
    quarter = tokens // 4
    sibling = place(zl, y, 1 - core, zh, x)

    barrier = pltpu.get_barrier_semaphore()
    partners = [
        sibling,
        place(zl, y, 0, beside, x), place(zl, y, 1, beside, x),
        place(zl, y, 0, across, x), place(zl, y, 1, across, x),
        place(zl, y, core, zh, right), place(zl, y, core, zh, left),
        place(zl, up_y, core, zh, x), place(zl, down_y, core, zh, x),
        place(1 - zl, y, core, zh, x), place(1 - zl, y, core, across, x),
    ]
    for partner in partners:
        pl.semaphore_signal(barrier, inc=1, device_id=partner)
    pl.semaphore_wait(barrier, len(partners))

    def remote(src, dst, send, recv, device):
        return pltpu.make_async_remote_copy(
            src_ref=src, dst_ref=dst, send_sem=send, recv_sem=recv, device_id=device)

    def block(m, zs, xs, start=0, rows=depth):
        return weights.at[m, pl.ds(zs * group + xs * depth + start, rows)]

    mats = (gate_hbm, up_hbm)

    def start_z(m, device, j, slot):
        return remote(mats[m], block(m, zh, x), z_send.at[slot], z_recv.at[j], device)

    def z_arrival(j):
        return remote(block(core, sources[j], x), block(core, sources[j], x),
                      z_send.at[3], z_recv.at[j], sibling)

    def in_copy(src_ref, q, start, rows, slot_send, slot_recv, device):
        at = pl.ds(q * quarter + start, rows)
        return remote(src_ref.at[at], acts.at[at], in_send.at[slot_send], in_recv.at[slot_recv], device)

    acts_copy = pltpu.make_async_copy(x_hbm, acts, local_sem.at[0])
    pin_copy = pltpu.make_async_copy(pin_hbm, pin, local_sem.at[1])
    pin_remote = remote(pin_hbm, pin, in_send.at[0], in_recv.at[0], sibling)
    quarter_out = in_copy(x_hbm, y, 0, quarter, 1, 1, place(1 - zl, y, core, across, x))
    quarter_on = in_copy(acts, y, 0, quarter, 2, 1, place(1 - zl, y, core, zh, x))
    quarter_up = in_copy(acts, y, 0, quarter, 3, 2, place(zl, up_y, core, zh, x))
    quarter_down = in_copy(acts, y, 0, quarter, 4, 3, place(zl, down_y, core, zh, x))
    half_up = in_copy(acts, down_y, 0, quarter // 2, 5, 4, place(zl, up_y, core, zh, x))
    half_down = in_copy(acts, up_y, quarter // 2, quarter // 2, 6, 5, place(zl, down_y, core, zh, x))

    for m in range(2):
        own_copy = pltpu.make_async_copy(mats[m], block(m, zh, x), local_sem.at[2])

        @pl.when(native & (core == m))
        def _():
            own_copy.start()

    @pl.when(native)
    def _():
        for m in range(2):

            @pl.when(core != m)
            def _():
                start_z(m, sibling, 0, 2).start()

        for m in range(2):
            start_z(m, place(zl, y, m, beside, x), 1, m).start()
        for m in range(2):

            @pl.when(core == m)
            def _():
                pltpu.make_async_copy(mats[m], block(m, zh, x), local_sem.at[2]).wait()

        pin_remote.start()
        pin_copy.start()
        acts_copy.start()

        @pl.when(next_to_across)
        def _():
            quarter_out.start()

    @pl.when(jnp.logical_not(native))
    def _():
        for m in range(2):
            start_z(m, place(zl, y, m, across, x), 2, m).start()
        z_arrival(0).wait_recv()

    def sib_copy(j, k):
        xs = (x, left, right, far)[k]
        return remote(block(core, sources[j], xs), block(core, sources[j], xs),
                      sib_send.at[j, k], sib_recv.at[j, k], sibling)

    def x_copy(j, k):
        zs = sources[j]
        half = depth // 2
        ref, device = {
            0: (block(core, zs, x), right),
            1: (block(core, zs, x), left),
            2: (block(core, zs, left, 0, half), right),
            3: (block(core, zs, right, half, half), left),
        }[k]
        return remote(ref, ref, x_send.at[j, k], x_recv.at[j, k], place(zl, y, core, zh, device))

    z_forward = remote(block(core, across, x), block(core, across, x),
                       z_send.at[3], z_recv.at[3], place(zl, y, core, beside, x))

    def have_column(j):
        if j > 0:
            z_arrival(j).wait_recv()
        if j == 2:
            z_forward.start()
        x_copy(j, 0).start()
        x_copy(j, 1).start()
        sib_copy(j, 0).start()

    def have_sides(j):
        for k in range(2):
            x_copy(j, k).wait_recv()
            x_copy(j, 2 + k).start()
            sib_copy(j, 1 + k).start()

    def have_far(j):
        x_copy(j, 2).wait_recv()
        x_copy(j, 3).wait_recv()
        sib_copy(j, 3).start()

    def sib_arrival(j):
        for k in range(4):
            xs = (x, left, right, far)[k]
            remote(block(1 - core, sources[j], xs), block(1 - core, sources[j], xs),
                   sib_send.at[j, k], sib_recv.at[j, k], sibling).wait_recv()

    def quarter_in():
        return remote(acts.at[pl.ds(y * quarter, quarter)], acts.at[pl.ds(y * quarter, quarter)],
                      in_send.at[1], in_recv.at[1], sibling)

    have_column(0)
    have_column(1)
    have_sides(0)
    have_column(2)

    @pl.when(jnp.logical_not(native))
    def _():
        quarter_in().wait_recv()

        @pl.when(next_to_across)
        def _():
            quarter_on.start()

        quarter_up.start()
        quarter_down.start()

    have_far(0)
    have_sides(1)
    have_column(3)
    have_far(1)
    have_sides(2)

    @pl.when(jnp.logical_not(native))
    def _():
        quarter_up.wait_recv()
        half_up.start()
        quarter_down.wait_recv()
        half_down.start()

    have_far(2)

    @pl.when(jnp.logical_not(native))
    def _():
        half_up.wait_recv()
        half_down.wait_recv()
        pin_remote.wait_recv()

    @pl.when(native)
    def _():
        acts_copy.wait()
        pin_copy.wait()

    tile = 256

    def products(j, t):
        rows = pl.ds(pl.multiple_of(t * tile, tile), tile)
        deep = pl.ds(pl.multiple_of(sources[j] * group, group), group)
        a = acts[rows, deep]
        gate = jnp.dot(a, weights[0, deep, :], preferred_element_type=jnp.float32)
        up = jnp.dot(a, weights[1, deep, :], preferred_element_type=jnp.float32)
        return rows, gate, up

    def compute(j):
        sib_arrival(j)

        def step(t, carry):
            rows, gate, up = products(j, t)
            if j == 0:
                acc_gate[rows, :] = gate
                acc_up[rows, :] = up
            else:
                acc_gate[rows, :] += gate
                acc_up[rows, :] += up
            return carry

        lax.fori_loop(0, tokens // tile, step, 0)

    compute(0)
    have_sides(3)
    compute(1)
    compute(2)
    have_far(3)
    sib_arrival(3)

    def finish(t, carry):
        rows, gate, up = products(3, t)
        gate = acc_gate[rows, :] + gate
        up = acc_up[rows, :] + up
        hidden = (gate / (1.0 + jnp.exp(-gate)) * up).astype(jnp.bfloat16)
        left_ref[:, rows] = lax.dot_general(
            pin[...], hidden, (((0,), (1,)), ((), ())), preferred_element_type=jnp.float32)
        return carry

    lax.fori_loop(0, tokens // tile, finish, 0)

    @pl.when(native)
    def _():
        for m in range(2):
            start_z(m, place(zl, y, m, beside, x), 1, m).wait_send()

            @pl.when(core != m)
            def _():
                start_z(m, sibling, 0, 2).wait_send()

        pin_remote.wait_send()

        @pl.when(next_to_across)
        def _():
            quarter_out.wait_send()

    @pl.when(jnp.logical_not(native))
    def _():
        for m in range(2):
            start_z(m, place(zl, y, m, across, x), 2, m).wait_send()

        @pl.when(next_to_across)
        def _():
            quarter_on.wait_send()

        quarter_up.wait_send()
        quarter_down.wait_send()
        half_up.wait_send()
        half_down.wait_send()

    z_forward.wait_send()
    for j in range(4):
        for k in range(4):
            x_copy(j, k).wait_send()
            sib_copy(j, k).wait_send()


def ffn(inputs, gate_weight, up_weight, proj_in):
    tokens, width = inputs.shape
    units = gate_weight.shape[1]
    f32, bf16 = jnp.float32, jnp.bfloat16
    dma = pltpu.SemaphoreType.DMA
    return pl.pallas_call(
        ffn_kernel,
        out_shape=jax.ShapeDtypeStruct((KIN, tokens), f32),
        in_specs=[pl.BlockSpec(memory_space=pl.ANY)] * 4,
        out_specs=pl.BlockSpec(memory_space=pltpu.VMEM),
        scratch_shapes=[
            pltpu.VMEM((2, width, units), bf16),
            pltpu.VMEM((tokens, width), bf16),
            pltpu.VMEM((tokens, units), f32),
            pltpu.VMEM((tokens, units), f32),
            pltpu.VMEM((units, KIN), bf16),
            dma((3,)),
            dma((4,)), dma((4,)),
            dma((4, 4)), dma((4, 4)),
            dma((4, 4)), dma((4, 4)),
            dma((7,)), dma((6,)),
        ],
        compiler_params=pltpu.CompilerParams(
            collective_id=2, has_side_effects=True, vmem_limit_bytes=56 * 1024 * 1024),
        name="ffn",
    )(inputs, gate_weight, up_weight, proj_in)


def tail_kernel(
    left_ref, cot_ref, pout_ref, fisher_ref, stored_ref, out_ref,
    right_part, right_recv, right_own, right_all, left_recv,
    grads_own, grads_all, part, part_recv, prec_all, part2, part2_recv,
    send_sem, recv_sem, local_sem,
):
    row = lax.axis_index("row")
    col = lax.axis_index("col")
    tokens = cot_ref.shape[0]
    tok_blk = tokens // N
    seqs = tokens // TOK_SEQ

    def row_dev(d):
        return {"row": lax.rem(row + d, N), "col": col}

    def col_dev(d):
        return {"row": row, "col": lax.rem(col + d, N)}

    x = lax.rem(col, 4)
    zh = col // 4
    kind = zh // 2
    core = lax.rem(row, 2)
    native = core == kind
    across = (3 - zh) * 4 + x
    target = jnp.where(native, col, across)

    barrier = pltpu.get_barrier_semaphore()

    def greet(d, carry):
        pl.semaphore_signal(barrier, inc=1, device_id=row_dev(d))
        pl.semaphore_signal(barrier, inc=1, device_id=col_dev(d))
        pl.semaphore_signal(barrier, inc=1, device_id={"row": lax.rem(row + d, N), "col": across})
        return carry

    lax.fori_loop(1, N, greet, 0)

    right_part[...] = jnp.dot(cot_ref[...], pout_ref[...], preferred_element_type=jnp.float32)
    pl.semaphore_wait(barrier, 3 * (N - 1))

    def exchange(phase, src_of, dst_of, dev_of):
        def copy(d):
            return pltpu.make_async_remote_copy(
                src_ref=src_of(d), dst_ref=dst_of(d),
                send_sem=send_sem.at[phase, d], recv_sem=recv_sem.at[phase, d],
                device_id=dev_of(d),
            )

        def start(d, carry):
            copy(d).start()
            return carry

        def wait_recv(d, carry):
            copy(d).wait_recv()
            return carry

        def wait_send(d, carry):
            copy(d).wait_send()
            return carry

        lax.fori_loop(1, N, start, 0)
        return (
            lambda: lax.fori_loop(1, N, wait_recv, 0),
            lambda: lax.fori_loop(1, N, wait_send, 0),
        )

    def at_row(d):
        return lax.rem(row + d, N)

    def at_col(d):
        return lax.rem(col + d, N)

    right_in, right_sent = exchange(
        0, lambda d: right_part.at[pl.ds(at_row(d) * tok_blk, tok_blk)],
        lambda d: right_recv.at[d], row_dev)
    slot = row - core + jnp.where(native, 0, 1)

    def left_copy(d):
        to = at_row(d)
        return pltpu.make_async_remote_copy(
            src_ref=left_ref.at[pl.ds(to * 8, 8)], dst_ref=left_recv.at[slot],
            send_sem=send_sem.at[1, d], recv_sem=recv_sem.at[1, slot],
            device_id={"row": to, "col": target})

    def left_start(d, carry):
        left_copy(d).start()
        return carry

    lax.fori_loop(1, N, left_start, 0)

    @pl.when(native)
    def _():
        own_left = pltpu.make_async_copy(
            left_ref.at[pl.ds(row * 8, 8)], left_recv.at[slot], local_sem)
        own_left.start()
        own_left.wait()

    @pl.when(jnp.logical_not(native))
    def _():
        left_copy(0).start()

    def left_in():
        def wait_one(s, carry):
            @pl.when(jnp.logical_not(native & (s == slot)))
            def _():
                pltpu.make_async_remote_copy(
                    src_ref=left_recv.at[s], dst_ref=left_recv.at[s],
                    send_sem=send_sem.at[1, 0], recv_sem=recv_sem.at[1, s],
                    device_id={"row": lax.rem(row + 1, N), "col": col}).wait_recv()

            return carry

        lax.fori_loop(0, N, wait_one, 0)

    def left_sent():
        def wait_one(d, carry):
            left_copy(d).wait_send()
            return carry

        lax.fori_loop(1, N, wait_one, 0)

        @pl.when(jnp.logical_not(native))
        def _():
            left_copy(0).wait_send()

    right_in()
    total = right_part[pl.ds(row * tok_blk, tok_blk), :]
    for d in range(1, N):
        total = total + right_recv[d]
    right_own[...] = total
    right_all[pl.ds(row * tok_blk, tok_blk), :] = total
    rall_in, rall_sent = exchange(
        2, lambda d: right_own,
        lambda d: right_all.at[pl.ds(row * tok_blk, tok_blk)], row_dev)

    left_in()
    left = left_recv[0]
    for d in range(1, N):
        left = left + left_recv[d]
    lane = lax.broadcasted_iota(jnp.int32, (PAD, tokens), 1)
    first = lax.broadcasted_iota(jnp.int32, (PAD, tokens), 0) * TOK_SEQ
    inside = (lane >= first) & (lane < first + TOK_SEQ)
    spread = jnp.concatenate(
        [jnp.where(inside, jnp.broadcast_to(left[i : i + 1, :], (PAD, tokens)), 0.0) for i in range(8)], axis=0)
    rall_in()
    grads = jnp.dot(spread, right_all[...], preferred_element_type=jnp.float32, precision=lax.Precision.HIGHEST)
    for i in range(8):
        piece = grads[i * PAD : (i + 1) * PAD, :].astype(jnp.bfloat16)
        grads_own[:, i * KOUT : (i + 1) * KOUT] = piece
        grads_all[pl.ds(pl.multiple_of(col * PAD, PAD), PAD), i * KOUT : (i + 1) * KOUT] = piece

    gall_in, gall_sent = exchange(
        3, lambda d: grads_own,
        lambda d: grads_all.at[pl.ds(col * PAD, PAD)], col_dev)
    gall_in()
    part[...] = jnp.dot(grads_all[...], fisher_ref[...], preferred_element_type=jnp.float32)
    part_in, part_sent = exchange(
        4, lambda d: part.at[pl.ds(at_row(d) * PAD, PAD)],
        lambda d: part_recv.at[d], row_dev)
    part_in()
    total = part[pl.ds(pl.multiple_of(row * PAD, PAD), PAD), :]
    for d in range(1, N):
        total = total + part_recv[d]
    own = total.astype(jnp.bfloat16)
    gall_sent()
    grads_own[...] = own
    prec_all[pl.ds(pl.multiple_of(row * PAD, PAD), PAD), :] = own
    pall_in, pall_sent = exchange(
        5, lambda d: grads_own,
        lambda d: prec_all.at[pl.ds(row * PAD, PAD)], row_dev)
    pall_in()
    part2[...] = lax.dot_general(
        prec_all[...], stored_ref[...], (((1,), (1,)), ((), ())), preferred_element_type=jnp.float32)
    part2_in, part2_sent = exchange(
        6, lambda d: part2.at[pl.ds(at_col(d) * PAD, PAD)],
        lambda d: part2_recv.at[d], col_dev)
    part2_in()
    total = part2[pl.ds(pl.multiple_of(col * PAD, PAD), PAD), :]
    for d in range(1, N):
        total = total + part2_recv[d]
    out_ref[...] = total[:seqs, :]
    for sent in (right_sent, left_sent, rall_sent, part_sent, pall_sent, part2_sent):
        sent()


def tail(left_t, cotangent, proj_out, fisher, stored):
    tokens = cotangent.shape[0]
    feats = fisher.shape[0]
    rows = N * PAD
    f32, bf16 = jnp.float32, jnp.bfloat16
    return pl.pallas_call(
        tail_kernel,
        out_shape=jax.ShapeDtypeStruct((tokens // TOK_SEQ, stored.shape[0]), f32),
        in_specs=[pl.BlockSpec(memory_space=pltpu.VMEM)] * 5,
        out_specs=pl.BlockSpec(memory_space=pltpu.VMEM),
        scratch_shapes=[
            pltpu.VMEM((tokens, KOUT), f32),
            pltpu.VMEM((N, tokens // N, KOUT), f32),
            pltpu.VMEM((tokens // N, KOUT), f32),
            pltpu.VMEM((tokens, KOUT), f32),
            pltpu.VMEM((N, 8, tokens), f32),
            pltpu.VMEM((PAD, feats), bf16),
            pltpu.VMEM((rows, feats), bf16),
            pltpu.VMEM((rows, feats), f32),
            pltpu.VMEM((N, PAD, feats), f32),
            pltpu.VMEM((rows, feats), bf16),
            pltpu.VMEM((rows, feats), f32),
            pltpu.VMEM((N, PAD, feats), f32),
            pltpu.SemaphoreType.DMA((7, N)),
            pltpu.SemaphoreType.DMA((7, N)),
            pltpu.SemaphoreType.DMA,
        ],
        compiler_params=pltpu.CompilerParams(
            collective_id=1, has_side_effects=True, vmem_limit_bytes=48 * 1024 * 1024),
        name="tail",
    )(left_t, cotangent, proj_out, fisher, stored)


def body(inputs, cotangent, gate_weight, up_weight, proj_in, proj_out, inverse_fisher, stored):
    left_t = ffn(inputs, gate_weight, up_weight, proj_in)
    return tail(left_t, cotangent, proj_out, inverse_fisher, stored)


def solution(mesh):
    return jax.shard_map(
        body,
        mesh=mesh,
        in_specs=(
            P("col", None),
            P("col", "row"),
            P("col", "row"),
            P("col", "row"),
            P("row", None),
            P("row", None),
            P("row", "col"),
            P("row", "col"),
        ),
        out_specs=P("col", "row"),
        check_vma=False,
    )
```

```python
import jax
import jax.numpy as jnp
from jax import lax
from jax.experimental import pallas as pl
from jax.experimental.pallas import tpu as pltpu
from jax.sharding import PartitionSpec as P

KIN = 128
KOUT = 128
TOK_SEQ = 64
N = 16
PAD = 16
TILE = 256


def place(zl, y, core, zh, x):
    return {"row": (zl * 4 + y) * 2 + core, "col": zh * 4 + x}


def remote(src, dst, send, recv, device):
    return pltpu.make_async_remote_copy(
        src_ref=src, dst_ref=dst, send_sem=send, recv_sem=recv, device_id=device)


def scores_kernel(
    x_hbm, cot_hbm, gate_hbm, up_hbm, pin_hbm, pout_hbm, fisher_hbm, stored_hbm, out_ref,
    weights, acts, acc_gate, acc_up, pin, cot, pout, fisher, stored,
    left_part, left_recv, right_part, right_recv, right_own, right_all,
    grads_all, part, part_recv, prec_own, prec_all, part2, part2_recv, fold, fold_recv,
    local_sem, z_send, z_recv, x_send, x_recv, sib_send, sib_recv, in_send, in_recv,
    tail_send, tail_recv,
):
    row = lax.axis_index("row")
    col = lax.axis_index("col")
    core = lax.rem(row, 2)
    y = lax.rem(row // 2, 4)
    zl = row // 8
    x = lax.rem(col, 4)
    zh = col // 4
    kind = zh // 2
    native = core == kind
    foreign = core != kind
    beside = zh + 1 - 2 * lax.rem(zh, 2)
    across = 3 - zh
    across_beside = across + 1 - 2 * lax.rem(across, 2)
    next_to_across = lax.rem(zh, 2) == zl
    sources = (zh, beside, across, across_beside)
    right = lax.rem(x + 1, 4)
    left = lax.rem(x + 3, 4)
    far = lax.rem(x + 2, 4)
    sides = (x, left, right, far)
    up_y = lax.rem(y + 1, 4)
    down_y = lax.rem(y + 3, 4)
    depth = gate_hbm.shape[0]
    sub = depth // 2
    group = 4 * depth
    tokens = x_hbm.shape[0]
    quarter = tokens // 4
    eighth = quarter // 2
    tok_blk = tokens // N
    seqs = tokens // TOK_SEQ
    sibling = place(zl, y, 1 - core, zh, x)
    token_col = jnp.where(native, zh, across) * 4 + x

    def row_dev(d):
        return {"row": lax.rem(row + d, N), "col": col}

    loads = [
        pltpu.make_async_copy(a, b, local_sem.at[i])
        for i, (a, b) in enumerate(
            [(cot_hbm, cot), (pout_hbm, pout), (fisher_hbm, fisher), (stored_hbm, stored)])
    ]
    acts_copy = pltpu.make_async_copy(x_hbm, acts, local_sem.at[4])
    pin_copy = pltpu.make_async_copy(pin_hbm, pin, local_sem.at[5])
    for load in loads:
        load.start()

    barrier = pltpu.get_barrier_semaphore()
    partners = [row_dev(d) for d in range(1, N)]
    partners += [{"row": lax.rem(row + d, N), "col": across * 4 + x} for d in range(N)]
    partners += [place(zl, y, 0, beside, x), place(zl, y, 1, beside, x), place(zl, y, core, across_beside, x)]
    partners += [place(zl, y, core, zh, side) for side in (right, left, far)]
    for partner in partners:
        pl.semaphore_signal(barrier, inc=1, device_id=partner)
    pl.semaphore_wait(barrier, len(partners))

    def block(m, zs, xs, start=0, rows=depth):
        return weights.at[m, pl.ds(zs * group + xs * depth + start, rows)]

    mats = (gate_hbm, up_hbm)

    def z_copy(m, s, device, j, slot):
        return remote(mats[m].at[pl.ds(s * sub, sub)], block(m, zh, x, s * sub, sub),
                      z_send.at[slot, s], z_recv.at[j, s], device)

    def z_forward(s):
        ref = block(core, across, x, s * sub, sub)
        return remote(ref, ref, z_send.at[3, s], z_recv.at[3, s], place(zl, y, core, beside, x))

    def z_arrival(j, s):
        ref = block(core, sources[j], x, s * sub, sub)
        return remote(ref, ref, z_send.at[3, s], z_recv.at[j, s], sibling)

    def in_copy(src_ref, q, s, slot, recv_slot, device):
        at = pl.ds(q * quarter + s * eighth, eighth)
        return remote(src_ref.at[at], acts.at[at], in_send.at[slot], in_recv.at[recv_slot], device)

    pin_remote = remote(pin_hbm, pin, in_send.at[0], in_recv.at[0], sibling)

    def quarter_out(s):
        return in_copy(x_hbm, y, s, 1 + s, 1 + s, place(1 - zl, y, core, across, x))

    def quarter_on(s):
        return in_copy(acts, y, s, 3 + s, 1 + s, place(1 - zl, y, core, zh, x))

    def quarter_up(s):
        return in_copy(acts, y, s, 5 + s, 5 + s, place(zl, up_y, core, zh, x))

    def quarter_down(s):
        return in_copy(acts, y, s, 7 + s, 7 + s, place(zl, down_y, core, zh, x))

    half_up = in_copy(acts, down_y, 0, 9, 9, place(zl, up_y, core, zh, x))
    half_down = in_copy(acts, up_y, 1, 10, 10, place(zl, down_y, core, zh, x))

    def own_copy(m):
        return pltpu.make_async_copy(mats[m], block(m, zh, x), local_sem.at[6])

    @pl.when(native)
    def _():
        for m in range(2):

            @pl.when(core == m)
            def _():
                own_copy(m).start()

            @pl.when(core != m)
            def _():
                for s in range(2):
                    z_copy(m, s, sibling, 0, 2).start()

        @pl.when(next_to_across)
        def _():
            for s in range(2):
                quarter_out(s).start()

        for s in range(2):
            for m in range(2):
                z_copy(m, s, place(zl, y, m, beside, x), 1, m).start()
        for m in range(2):

            @pl.when(core == m)
            def _():
                own_copy(m).wait()

        pin_remote.start()
        pin_copy.start()
        acts_copy.start()

    def across_start(s):
        @pl.when(foreign)
        def _():
            for m in range(2):
                z_copy(m, s, place(zl, y, m, across, x), 2, m).start()

    def sib_copy(j, k):
        ref = block(core, sources[j], sides[k])
        return remote(ref, ref, sib_send.at[j, k], sib_recv.at[j, k], sibling)

    def x_copy(j, k):
        side, s = (k // 2, k % 2) if k < 4 else (k - 4, k - 4)
        whose = x if k < 4 else (left, right)[side]
        ref = block(core, sources[j], whose, s * sub, sub)
        return remote(ref, ref, x_send.at[j, k], x_recv.at[j, k],
                      place(zl, y, core, zh, (right, left)[side]))

    def have_column(j, s):
        if j > 0:
            z_arrival(j, s).wait_recv()
        else:

            @pl.when(foreign)
            def _():
                z_arrival(0, s).wait_recv()

        if j == 2:
            z_forward(s).start()
        x_copy(j, s).start()
        x_copy(j, 2 + s).start()
        if s == 1:
            sib_copy(j, 0).start()

    def have_side(j, s):
        for side in range(2):
            x_copy(j, 2 * side + s).wait_recv()
            if s == side:
                x_copy(j, 4 + s).start()
            if s == 1:
                sib_copy(j, 1 + side).start()

    def have_far(j):
        x_copy(j, 4).wait_recv()
        x_copy(j, 5).wait_recv()
        sib_copy(j, 3).start()

    def sib_arrival(j, k):
        ref = block(1 - core, sources[j], sides[k])
        remote(ref, ref, sib_send.at[j, k], sib_recv.at[j, k], sibling).wait_recv()

    def have_quarter(s):
        @pl.when(foreign)
        def _():
            quarter_out(s).wait_recv()

            @pl.when(next_to_across)
            def _():
                quarter_on(s).start()

            quarter_up(s).start()
            quarter_down(s).start()

    def pass_quarters():
        @pl.when(foreign)
        def _():
            quarter_up(0).wait_recv()
            half_up.start()
            quarter_up(1).wait_recv()
            quarter_down(0).wait_recv()
            quarter_down(1).wait_recv()
            half_down.start()

    def have_inputs():
        @pl.when(foreign)
        def _():
            half_up.wait_recv()
            half_down.wait_recv()
            pin_remote.wait_recv()

        @pl.when(native)
        def _():
            acts_copy.wait()
            pin_copy.wait()

    def many(phase, src_of, dst_of, dev_of, first=1, last=N):
        def copy(d):
            return remote(src_of(d), dst_of(d), tail_send.at[phase, d], tail_recv.at[phase, d], dev_of(d))

        def run(action):
            def step(d, carry):
                action(copy(d))
                return carry

            lax.fori_loop(first, last, step, 0)

        run(lambda c: c.start())
        return lambda: run(lambda c: c.wait_recv()), lambda: run(lambda c: c.wait_send())

    def at_row(d):
        return lax.rem(row + d, N)

    def deep_dot(j, rows, start=0, size=group):
        deep = pl.ds(pl.multiple_of(sources[j] * group + start, 256), size)
        a = acts[rows, deep]
        return (jnp.dot(a, weights[0, deep, :], preferred_element_type=jnp.float32),
                jnp.dot(a, weights[1, deep, :], preferred_element_type=jnp.float32))

    def tiles(step):
        def at(t, carry):
            step(pl.ds(pl.multiple_of(t * TILE, TILE), TILE))
            return carry

        lax.fori_loop(0, tokens // TILE, at, 0)

    def compute_first():
        def step(rows):
            gate, up = deep_dot(0, rows)
            acc_gate[rows, :] = gate
            acc_up[rows, :] = up

        tiles(step)

    def compute_add(j):
        def step(rows):
            gate, up = deep_dot(j, rows)
            acc_gate[rows, :] += gate
            acc_up[rows, :] += up

        tiles(step)

    def sibs(j):
        for k in range(4):
            sib_arrival(j, k)

    have_column(0, 0)
    have_column(0, 1)
    loads[0].wait()
    loads[1].wait()
    right_part[...] = jnp.dot(cot[...], pout[...], preferred_element_type=jnp.float32)
    right_in, right_sent = many(
        0, lambda d: right_part.at[pl.ds(at_row(d) * tok_blk, tok_blk)],
        lambda d: right_recv.at[d], row_dev)
    have_side(0, 0)
    across_start(0)
    have_quarter(0)
    have_column(1, 0)
    have_side(0, 1)
    across_start(1)
    have_quarter(1)
    have_column(1, 1)
    have_far(0)
    have_column(2, 0)
    have_side(1, 0)
    have_side(1, 1)
    have_column(2, 1)

    right_in()
    total = right_part[pl.ds(row * tok_blk, tok_blk), :]
    for d in range(1, N):
        total = total + right_recv[d]
    right_own[...] = total
    right_all[pl.ds(row * tok_blk, tok_blk), :] = total
    rall_in, rall_sent = many(
        2, lambda d: right_own,
        lambda d: right_all.at[pl.ds(row * tok_blk, tok_blk)], row_dev)

    have_column(3, 0)
    pass_quarters()
    have_far(1)
    have_side(2, 0)
    have_side(2, 1)
    have_column(3, 1)
    have_inputs()
    sibs(0)
    compute_first()
    have_far(2)
    have_side(3, 0)
    have_side(3, 1)
    sibs(1)
    compute_add(1)
    sibs(2)
    compute_add(2)
    have_far(3)
    sibs(3)

    def finish(rows):
        gate, up = deep_dot(3, rows)
        gate = acc_gate[rows, :] + gate
        up = acc_up[rows, :] + up
        hidden = (gate / (1.0 + jnp.exp(-gate)) * up).astype(jnp.bfloat16)
        left_part[:, rows] = lax.dot_general(
            pin[...], hidden, (((0,), (1,)), ((), ())), preferred_element_type=jnp.float32)

    tiles(finish)

    slot = row - core + jnp.where(native, 0, 1)

    def left_copy(d):
        to = at_row(d)
        return remote(left_part.at[pl.ds(to * 8, 8)], left_recv.at[slot],
                      tail_send.at[1, d], tail_recv.at[1, slot], {"row": to, "col": token_col})

    def left_start(d, carry):
        left_copy(d).start()
        return carry

    lax.fori_loop(1, N, left_start, 0)

    @pl.when(native)
    def _():
        left_recv[pl.ds(slot, 1)] = left_part[pl.ds(row * 8, 8), :][None]

    @pl.when(foreign)
    def _():
        left_copy(0).start()

    rall_in()

    def left_wait(s, carry):
        @pl.when(foreign | (s != slot))
        def _():
            remote(left_recv.at[s], left_recv.at[s], tail_send.at[1, 0], tail_recv.at[1, s], sibling).wait_recv()

        return carry

    lax.fori_loop(0, N, left_wait, 0)
    total = left_recv[0]
    for d in range(1, N):
        total = total + left_recv[d]
    lane = lax.broadcasted_iota(jnp.int32, (PAD, tokens), 1)
    first = lax.broadcasted_iota(jnp.int32, (PAD, tokens), 0) * TOK_SEQ
    inside = (lane >= first) & (lane < first + TOK_SEQ)
    spread = jnp.concatenate(
        [jnp.where(inside, jnp.broadcast_to(total[i : i + 1, :], (PAD, tokens)), 0.0) for i in range(8)], axis=0)
    grads = jnp.dot(spread, right_all[...], preferred_element_type=jnp.float32, precision=lax.Precision.HIGHEST)
    mine = pl.ds(pl.multiple_of((x * 4 + zh) * PAD, PAD), PAD)
    column = pl.ds(pl.multiple_of(x * 4 * PAD, PAD), 4 * PAD)
    for i in range(8):
        grads_all[mine, i * KOUT : (i + 1) * KOUT] = grads[i * PAD : (i + 1) * PAD, :].astype(jnp.bfloat16)

    def z_dev(d):
        return place(zl, y, core, lax.rem(zh + d, 4), x)

    def x_dev(d):
        return place(zl, y, core, zh, lax.rem(x + d, 4))

    gz_in, gz_sent = many(3, lambda d: grads_all.at[mine], lambda d: grads_all.at[mine], z_dev, 1, 4)
    gz_in()
    gx_in, gx_sent = many(
        3, lambda d: grads_all.at[column], lambda d: grads_all.at[column], lambda d: x_dev(d - 3), 4, 7)
    loads[2].wait()
    gx_in()
    part[...] = jnp.dot(
        grads_all[...], fisher[...], preferred_element_type=jnp.float32).astype(jnp.bfloat16)
    part_in, part_sent = many(
        4, lambda d: part.at[pl.ds(at_row(d) * PAD, PAD)],
        lambda d: part_recv.at[d], row_dev)
    row_rows = pl.ds(pl.multiple_of(row * PAD, PAD), PAD)
    part_in()
    total = part[row_rows, :].astype(jnp.float32)
    for d in range(1, N):
        total = total + part_recv[d].astype(jnp.float32)
    prec_own[...] = total.astype(jnp.bfloat16)
    prec_all[row_rows, :] = total.astype(jnp.bfloat16)
    pall_in, pall_sent = many(
        5, lambda d: prec_own, lambda d: prec_all.at[pl.ds(row * PAD, PAD)], row_dev)
    loads[3].wait()
    pall_in()
    part2[...] = lax.dot_general(
        prec_all[...], stored[...], (((1,), (1,)), ((), ())), preferred_element_type=jnp.float32).astype(jnp.bfloat16)
    sx_in, sx_sent = many(
        6, lambda d: part2.at[pl.ds(lax.rem(x + d, 4) * 4 * PAD, 4 * PAD)],
        lambda d: part2_recv.at[d], x_dev, 1, 4)
    sx_in()
    total = part2[column, :].astype(jnp.float32)
    for d in range(1, 4):
        total = total + part2_recv[d].astype(jnp.float32)
    fold[...] = total
    sz_in, sz_sent = many(
        6, lambda d: fold.at[pl.ds(lax.rem(zh + d - 3, 4) * PAD, PAD)],
        lambda d: fold_recv.at[d - 3], lambda d: z_dev(d - 3), 4, 7)
    sz_in()
    total = fold[pl.ds(pl.multiple_of(zh * PAD, PAD), PAD), :]
    for d in range(1, 4):
        total = total + fold_recv[d]
    out_ref[...] = total[:seqs, :]

    @pl.when(native)
    def _():
        for m in range(2):
            for s in range(2):
                z_copy(m, s, place(zl, y, m, beside, x), 1, m).wait_send()

                @pl.when(core != m)
                def _():
                    z_copy(m, s, sibling, 0, 2).wait_send()

        pin_remote.wait_send()

        @pl.when(next_to_across)
        def _():
            for s in range(2):
                quarter_out(s).wait_send()

    @pl.when(foreign)
    def _():
        for s in range(2):
            for m in range(2):
                z_copy(m, s, place(zl, y, m, across, x), 2, m).wait_send()

            @pl.when(next_to_across)
            def _():
                quarter_on(s).wait_send()

            quarter_up(s).wait_send()
            quarter_down(s).wait_send()
        half_up.wait_send()
        half_down.wait_send()
        left_copy(0).wait_send()

    for s in range(2):
        z_forward(s).wait_send()
    for j in range(4):
        for k in range(6):
            x_copy(j, k).wait_send()
        for k in range(4):
            sib_copy(j, k).wait_send()

    def left_done(d, carry):
        left_copy(d).wait_send()
        return carry

    lax.fori_loop(1, N, left_done, 0)
    for sent in (right_sent, rall_sent, gz_sent, gx_sent, part_sent, pall_sent, sx_sent, sz_sent):
        sent()


def body(inputs, cotangent, gate_weight, up_weight, proj_in, proj_out, inverse_fisher, stored):
    tokens, width = inputs.shape
    units = gate_weight.shape[1]
    feats, wide = inverse_fisher.shape
    rows = N * PAD
    f32, bf16 = jnp.float32, jnp.bfloat16
    dma = pltpu.SemaphoreType.DMA
    return pl.pallas_call(
        scores_kernel,
        out_shape=jax.ShapeDtypeStruct((tokens // TOK_SEQ, stored.shape[0]), f32),
        in_specs=[pl.BlockSpec(memory_space=pl.ANY)] * 8,
        out_specs=pl.BlockSpec(memory_space=pltpu.VMEM),
        scratch_shapes=[
            pltpu.VMEM((2, width, units), bf16),
            pltpu.VMEM((tokens, width), bf16),
            pltpu.VMEM((tokens, units), f32),
            pltpu.VMEM((tokens, units), f32),
            pltpu.VMEM((units, KIN), bf16),
            pltpu.VMEM(cotangent.shape, bf16),
            pltpu.VMEM(proj_out.shape, bf16),
            pltpu.VMEM(inverse_fisher.shape, bf16),
            pltpu.VMEM(stored.shape, bf16),
            pltpu.VMEM((KIN, tokens), f32),
            pltpu.VMEM((N, 8, tokens), f32),
            pltpu.VMEM((tokens, KOUT), f32),
            pltpu.VMEM((N, tokens // N, KOUT), f32),
            pltpu.VMEM((tokens // N, KOUT), f32),
            pltpu.VMEM((tokens, KOUT), f32),
            pltpu.VMEM((rows, feats), bf16),
            pltpu.VMEM((rows, wide), bf16),
            pltpu.VMEM((N, PAD, wide), bf16),
            pltpu.VMEM((PAD, wide), bf16),
            pltpu.VMEM((rows, wide), bf16),
            pltpu.VMEM((rows, stored.shape[0]), bf16),
            pltpu.VMEM((4, 4 * PAD, stored.shape[0]), bf16),
            pltpu.VMEM((4 * PAD, stored.shape[0]), f32),
            pltpu.VMEM((4, PAD, stored.shape[0]), f32),
            dma((7,)),
            dma((4, 2)), dma((4, 2)),
            dma((4, 6)), dma((4, 6)),
            dma((4, 4)), dma((4, 4)),
            dma((11,)), dma((11,)),
            dma((7, N)), dma((7, N)),
        ],
        compiler_params=pltpu.CompilerParams(
            collective_id=1, has_side_effects=True, vmem_limit_bytes=60 * 1024 * 1024),
        name="scores",
    )(inputs, cotangent, gate_weight, up_weight, proj_in, proj_out, inverse_fisher, stored)


def solution(mesh):
    return jax.shard_map(
        body,
        mesh=mesh,
        in_specs=(
            P("col", None),
            P("col", "row"),
            P("col", "row"),
            P("col", "row"),
            P("row", None),
            P("row", None),
            P("row", "col"),
            P("row", "col"),
        ),
        out_specs=P("col", "row"),
        check_vma=False,
    )
```

```python
import jax
import jax.numpy as jnp
from jax import lax
from jax.experimental import pallas as pl
from jax.experimental.pallas import tpu as pltpu
from jax.sharding import PartitionSpec as P

KIN = 128
KOUT = 128
TOK_SEQ = 64
N = 16
PAD = 16
TILE = 256


def place(zl, y, core, zh, x):
    return {"row": (zl * 4 + y) * 2 + core, "col": zh * 4 + x}


def remote(src, dst, send, recv, device):
    return pltpu.make_async_remote_copy(
        src_ref=src, dst_ref=dst, send_sem=send, recv_sem=recv, device_id=device)


def scores_kernel(
    x_hbm, cot_hbm, gate_hbm, up_hbm, pin_hbm, pout_hbm, fisher_hbm, stored_hbm, out_ref,
    weights, acts, acc_gate, acc_up, pin, cot, pout, fisher, stored,
    left_part, left_recv, right_part, right_recv, right_own, right_all,
    grads_all, packed, part, part_recv, prec_own, prec_all, part2, part2_recv, fold, fold_recv,
    local_sem, z_send, z_recv, x_send, x_recv, sib_send, sib_recv, in_send, in_recv,
    tail_send, tail_recv,
):
    row = lax.axis_index("row")
    col = lax.axis_index("col")
    core = lax.rem(row, 2)
    y = lax.rem(row // 2, 4)
    zl = row // 8
    x = lax.rem(col, 4)
    zh = col // 4
    kind = zh // 2
    native = core == kind
    foreign = core != kind
    beside = zh + 1 - 2 * lax.rem(zh, 2)
    across = 3 - zh
    across_beside = across + 1 - 2 * lax.rem(across, 2)
    next_to_across = lax.rem(zh, 2) == zl
    sources = (zh, beside, across, across_beside)
    right = lax.rem(x + 1, 4)
    left = lax.rem(x + 3, 4)
    far = lax.rem(x + 2, 4)
    sides = (x, left, right, far)
    up_y = lax.rem(y + 1, 4)
    down_y = lax.rem(y + 3, 4)
    depth = gate_hbm.shape[0]
    sub = depth // 2
    group = 4 * depth
    tokens = x_hbm.shape[0]
    quarter = tokens // 4
    slab = quarter // 4
    tok_blk = tokens // N
    seqs = tokens // TOK_SEQ
    high = 4 * seqs
    broad = fisher.shape[1] // 4
    sibling = place(zl, y, 1 - core, zh, x)
    token_col = jnp.where(native, zh, across) * 4 + x

    def row_dev(d):
        return {"row": lax.rem(row + d, N), "col": col}

    loads = [
        pltpu.make_async_copy(a, b, local_sem.at[i])
        for i, (a, b) in enumerate(
            [(cot_hbm, cot), (pout_hbm, pout), (fisher_hbm, fisher), (stored_hbm, stored)])
    ]
    acts_copy = pltpu.make_async_copy(x_hbm, acts, local_sem.at[4])
    pin_copy = pltpu.make_async_copy(pin_hbm, pin, local_sem.at[5])
    for load in loads:
        load.start()

    fold[...] = jnp.zeros_like(fold)
    barrier = pltpu.get_barrier_semaphore()
    partners = [{"row": lax.rem(row + d, N), "col": across * 4 + x} for d in range(N)]
    partners += [place(zl, y, core, across_beside, x)]
    partners += [place(zl, y, core, zh, side) for side in (far, right, left)]
    partners += [place(zl, y, 0, beside, x), place(zl, y, 1, beside, x)]
    partners += [row_dev(d) for d in range(1, N)]
    for partner in partners:
        pl.semaphore_signal(barrier, inc=1, device_id=partner)
    pl.semaphore_wait(barrier, len(partners))

    def block(m, zs, xs, start=0, rows=depth):
        return weights.at[m, pl.ds(zs * group + xs * depth + start, rows)]

    mats = (gate_hbm, up_hbm)

    def z_copy(m, s, device, j, slot):
        return remote(mats[m].at[pl.ds(s * sub, sub)], block(m, zh, x, s * sub, sub),
                      z_send.at[slot, s], z_recv.at[j, s], device)

    def z_forward(s):
        ref = block(core, across, x, s * sub, sub)
        return remote(ref, ref, z_send.at[3, s], z_recv.at[3, s], place(zl, y, core, beside, x))

    def z_arrival(j, s):
        ref = block(core, sources[j], x, s * sub, sub)
        return remote(ref, ref, z_send.at[3, s], z_recv.at[j, s], sibling)

    def in_copy(src_ref, q, s, slot, recv_slot, device):
        at = pl.ds(q * quarter + s * slab, slab)
        return remote(src_ref.at[at], acts.at[at], in_send.at[slot], in_recv.at[recv_slot], device)

    pin_remote = remote(pin_hbm, pin, in_send.at[0], in_recv.at[0], sibling)

    def quarter_out(s):
        return in_copy(x_hbm, y, s, 1 + s, 1 + s, place(1 - zl, y, core, across, x))

    def quarter_on(s):
        return in_copy(acts, y, s, 5 + s, 1 + s, place(1 - zl, y, core, zh, x))

    def quarter_up(s):
        return in_copy(acts, y, s, 9 + s, 9 + s, place(zl, up_y, core, zh, x))

    def quarter_down(s):
        return in_copy(acts, y, s, 13 + s, 13 + s, place(zl, down_y, core, zh, x))

    def far_quarter(s):
        if s < 2:
            return in_copy(acts, down_y, s, 17 + s, 17 + s, place(zl, up_y, core, zh, x))
        return in_copy(acts, up_y, s, 17 + s, 17 + s, place(zl, down_y, core, zh, x))

    def own_copy(m):
        return pltpu.make_async_copy(mats[m], block(m, zh, x), local_sem.at[6])

    @pl.when(native)
    def _():
        for m in range(2):

            @pl.when(core == m)
            def _():
                own_copy(m).start()

            @pl.when(core != m)
            def _():
                for s in range(2):
                    z_copy(m, s, sibling, 0, 2).start()

        @pl.when(next_to_across)
        def _():
            for s in range(4):
                quarter_out(s).start()

        for s in range(2):
            for m in range(2):
                z_copy(m, s, place(zl, y, m, beside, x), 1, m).start()
        for m in range(2):

            @pl.when(core == m)
            def _():
                own_copy(m).wait()

        pin_remote.start()
        pin_copy.start()
        acts_copy.start()

    def across_start(s):
        @pl.when(foreign)
        def _():
            for m in range(2):
                z_copy(m, s, place(zl, y, m, across, x), 2, m).start()

    def sib_copy(j, k):
        ref = block(core, sources[j], sides[k])
        return remote(ref, ref, sib_send.at[j, k], sib_recv.at[j, k], sibling)

    def x_copy(j, k):
        side, s = (k // 2, k % 2) if k < 4 else (k - 4, k - 4)
        whose = x if k < 4 else (left, right)[side]
        ref = block(core, sources[j], whose, s * sub, sub)
        return remote(ref, ref, x_send.at[j, k], x_recv.at[j, k],
                      place(zl, y, core, zh, (right, left)[side]))

    def have_column(j, s):
        if j > 0:
            z_arrival(j, s).wait_recv()
        else:

            @pl.when(foreign)
            def _():
                z_arrival(0, s).wait_recv()

        if j == 2:
            z_forward(s).start()
        x_copy(j, s).start()
        x_copy(j, 2 + s).start()
        if s == 1:
            sib_copy(j, 0).start()

    def have_side(j, s):
        for side in range(2):
            x_copy(j, 2 * side + s).wait_recv()
            if s == side:
                x_copy(j, 4 + s).start()
            if s == 1:
                sib_copy(j, 1 + side).start()

    def have_far(j):
        x_copy(j, 4).wait_recv()
        x_copy(j, 5).wait_recv()
        sib_copy(j, 3).start()

    def sib_arrival(j, k):
        ref = block(1 - core, sources[j], sides[k])
        remote(ref, ref, sib_send.at[j, k], sib_recv.at[j, k], sibling).wait_recv()

    def have_quarter(s):
        @pl.when(foreign)
        def _():
            quarter_out(s).wait_recv()

            @pl.when(next_to_across)
            def _():
                quarter_on(s).start()

            quarter_up(s).start()
            quarter_down(s).start()

    def pass_quarter(s):
        @pl.when(foreign)
        def _():
            quarter_up(s).wait_recv()
            quarter_down(s).wait_recv()
            far_quarter(s).start()

    def have_inputs():
        @pl.when(foreign)
        def _():
            for s in range(4):
                far_quarter(s).wait_recv()
            pin_remote.wait_recv()

        @pl.when(native)
        def _():
            pin_copy.wait()

    def own_kind():
        @pl.when(native)
        def _():
            acts_copy.wait()

    def many(phase, src_of, dst_of, dev_of, first=1, last=N):
        def copy(d):
            return remote(src_of(d), dst_of(d), tail_send.at[phase, d], tail_recv.at[phase, d], dev_of(d))

        def run(action):
            def step(d, carry):
                action(copy(d))
                return carry

            lax.fori_loop(first, last, step, 0)

        run(lambda c: c.start())
        return lambda: run(lambda c: c.wait_recv()), lambda: run(lambda c: c.wait_send())

    def at_row(d):
        return lax.rem(row + d, N)

    def deep_dot(rows, start, size):
        deep = pl.ds(pl.multiple_of(start, 256), size)
        a = acts[rows, deep]
        return (jnp.dot(a, weights[0, deep, :], preferred_element_type=jnp.float32),
                jnp.dot(a, weights[1, deep, :], preferred_element_type=jnp.float32))

    def group_dot(j, rows):
        return deep_dot(rows, sources[j] * group, group)

    def piece_dot(j, k, rows):
        return deep_dot(rows, sources[j] * group + sides[k] * depth, depth)

    def tiles(step):
        def at(t, carry):
            step(pl.ds(pl.multiple_of(t * TILE, TILE), TILE))
            return carry

        lax.fori_loop(0, tokens // TILE, at, 0)

    def quarter_rows(ahead):
        return pl.ds(pl.multiple_of(lax.rem(y + ahead, 4) * quarter, 64), quarter)

    def compute_near(j):
        def step(t, carry):
            rows = quarter_rows(t + t // 2)
            gate, up = group_dot(j, rows)
            if j == 0:
                acc_gate[rows, :] = gate
                acc_up[rows, :] = up
            else:
                acc_gate[rows, :] += gate
                acc_up[rows, :] += up
            return carry

        lax.fori_loop(0, 3, step, 0)

    def compute_last():
        rows = quarter_rows(2)
        gate0, up0 = group_dot(0, rows)
        gate1, up1 = group_dot(1, rows)
        acc_gate[rows, :] = gate0 + gate1
        acc_up[rows, :] = up0 + up1

    def compute_add(j):
        def step(rows):
            gate, up = group_dot(j, rows)
            acc_gate[rows, :] += gate
            acc_up[rows, :] += up

        tiles(step)

    def compute_pieces(j):
        def step(rows):
            for m, acc in ((0, acc_gate), (1, acc_up)):
                total = acc[rows, :]
                for k in range(3):
                    deep = pl.ds(pl.multiple_of(sources[j] * group + sides[k] * depth, 256), depth)
                    total = total + jnp.dot(acts[rows, deep], weights[m, deep, :], preferred_element_type=jnp.float32)
                acc[rows, :] = total

        tiles(step)

    def sibs(j, first=0, last=4):
        for k in range(first, last):
            sib_arrival(j, k)

    have_column(0, 0)
    have_column(0, 1)
    loads[0].wait()
    loads[1].wait()
    right_part[...] = jnp.dot(cot[...], pout[...], preferred_element_type=jnp.float32)
    right_in, right_sent = many(
        0, lambda d: right_part.at[pl.ds(at_row(d) * tok_blk, tok_blk)],
        lambda d: right_recv.at[d], row_dev)
    have_side(0, 0)
    across_start(0)
    have_quarter(0)
    have_side(0, 1)
    across_start(1)
    have_column(1, 0)
    have_quarter(1)
    have_far(0)
    have_column(1, 1)
    have_quarter(2)
    pass_quarter(0)
    have_column(2, 0)
    have_side(1, 0)
    have_quarter(3)
    pass_quarter(1)
    have_side(1, 1)
    have_column(2, 1)
    right_in()
    total = right_part[pl.ds(row * tok_blk, tok_blk), :]
    for d in range(1, N):
        total = total + right_recv[d]
    right_own[...] = total
    right_all[pl.ds(row * tok_blk, tok_blk), :] = total
    rall_in, rall_sent = many(
        2, lambda d: right_own,
        lambda d: right_all.at[pl.ds(row * tok_blk, tok_blk)], row_dev)

    pass_quarter(2)
    have_far(1)
    have_column(3, 0)
    pass_quarter(3)
    have_side(2, 0)
    have_column(3, 1)
    have_side(2, 1)
    own_kind()
    sibs(0)
    compute_near(0)
    sibs(1)
    compute_near(1)
    have_inputs()
    compute_last()
    have_far(2)
    have_side(3, 0)
    sibs(2)
    compute_add(2)
    have_side(3, 1)
    sibs(3, 0, 3)
    compute_pieces(3)
    have_far(3)
    sibs(3, 3, 4)

    def finish(rows):
        gate, up = piece_dot(3, 3, rows)
        gate = acc_gate[rows, :] + gate
        up = acc_up[rows, :] + up
        hidden = (gate / (1.0 + jnp.exp(-gate)) * up).astype(jnp.bfloat16)
        left_part[:, rows] = lax.dot_general(
            pin[...], hidden, (((0,), (1,)), ((), ())), preferred_element_type=jnp.float32)

    tiles(finish)

    slot = row - core + jnp.where(native, 0, 1)

    def left_copy(d):
        to = at_row(d)
        return remote(left_part.at[pl.ds(to * 8, 8)], left_recv.at[slot],
                      tail_send.at[1, d], tail_recv.at[1, slot], {"row": to, "col": token_col})

    def left_start(d, carry):
        left_copy(d).start()
        return carry

    lax.fori_loop(1, N, left_start, 0)

    @pl.when(native)
    def _():
        left_recv[pl.ds(slot, 1)] = left_part[pl.ds(row * 8, 8), :][None]

    @pl.when(foreign)
    def _():
        left_copy(0).start()

    rall_in()

    def left_wait(s, carry):
        @pl.when(foreign | (s != slot))
        def _():
            remote(left_recv.at[s], left_recv.at[s], tail_send.at[1, 0], tail_recv.at[1, s], sibling).wait_recv()

        return carry

    lax.fori_loop(0, N, left_wait, 0)
    total = left_recv[0]
    for d in range(1, N):
        total = total + left_recv[d]
    lane = lax.broadcasted_iota(jnp.int32, (PAD, tokens), 1)
    first = lax.broadcasted_iota(jnp.int32, (PAD, tokens), 0) * TOK_SEQ
    inside = (lane >= first) & (lane < first + TOK_SEQ)
    spread = jnp.concatenate(
        [jnp.where(inside, jnp.broadcast_to(total[i : i + 1, :], (PAD, tokens)), 0.0) for i in range(8)], axis=0)
    grads = jnp.dot(spread, right_all[...], preferred_element_type=jnp.float32, precision=lax.Precision.HIGHEST)
    mine = pl.ds(pl.multiple_of((x * 4 + zh) * PAD, PAD), PAD)
    for i in range(8):
        grads_all[mine, i * KOUT : (i + 1) * KOUT] = grads[i * PAD : (i + 1) * PAD, :].astype(jnp.bfloat16)

    def z_dev(d):
        return place(zl, y, core, lax.rem(zh + d, 4), x)

    def x_dev(d):
        return place(zl, y, core, zh, lax.rem(x + d, 4))

    def grads_z(d):
        return remote(grads_all.at[mine], grads_all.at[mine], tail_send.at[3, d], tail_recv.at[3, d], z_dev(d))

    def grads_x(d, e):
        at = grads_all.at[pl.ds((x * 4 + lax.rem(zh + 4 - d, 4)) * PAD, PAD)]
        return remote(at, at, tail_send.at[7, d * 3 + e - 1], tail_recv.at[7, d * 3 + e - 1], x_dev(e))

    for d in (2, 1, 3):
        grads_z(d).start()
    for d in (0, 1, 3, 2):
        if d > 0:
            grads_z(d).wait_recv()
        for e in (2, 1, 3):
            grads_x(d, e).start()
    loads[2].wait()
    for d in (0, 1, 3, 2):
        for e in (1, 3, 2):
            grads_x(d, e).wait_recv()
    padded = jnp.dot(grads_all[...], fisher[...], preferred_element_type=jnp.float32)
    for b in range(N):
        packed[b * seqs : (b + 1) * seqs, :] = padded[b * PAD : b * PAD + seqs, :]
    part[...] = packed[...].astype(jnp.bfloat16)

    def piece(r):
        return (pl.ds(pl.multiple_of(r // 4 * high, high), high), pl.ds(pl.multiple_of(lax.rem(r, 4) * broad, broad), broad))

    part_in, part_sent = many(4, lambda d: part.at[piece(at_row(d))], lambda d: part_recv.at[d], row_dev)
    part_in()
    total = part[piece(row)].astype(jnp.float32)
    for d in range(1, N):
        total = total + part_recv[d].astype(jnp.float32)
    prec_own[...] = total.astype(jnp.bfloat16)
    prec_all[piece(row)] = total.astype(jnp.bfloat16)
    pall_in, pall_sent = many(5, lambda d: prec_own, lambda d: prec_all.at[piece(row)], row_dev)
    loads[3].wait()
    pall_in()
    span = stored.shape[0] // 2
    column = pl.ds(pl.multiple_of(x * high, high), high)

    def sum_x(h, d):
        return remote(
            part2.at[pl.ds(lax.rem(x + d, 4) * high, high), pl.ds(h * span, span)],
            part2_recv.at[d, :, pl.ds(h * span, span)],
            tail_send.at[6, h * 8 + d], tail_recv.at[6, h * 8 + d], x_dev(d))

    def sum_z(h, d):
        return remote(
            fold.at[lax.rem(zh + d, 4), :, pl.ds(h * span, span)],
            fold_recv.at[d, :, pl.ds(h * span, span)],
            tail_send.at[6, h * 8 + 4 + d], tail_recv.at[6, h * 8 + 4 + d], z_dev(d))

    for h in range(2):
        cols = slice(h * span, (h + 1) * span)
        part2[:, cols] = lax.dot_general(
            prec_all[...], stored[cols, :], (((1,), (1,)), ((), ())),
            preferred_element_type=jnp.float32).astype(jnp.bfloat16)
        for d in (2, 1, 3):
            sum_x(h, d).start()
    for h in range(2):
        cols = slice(h * span, (h + 1) * span)
        total = part2[column, cols].astype(jnp.float32)
        for d in (1, 3, 2):
            sum_x(h, d).wait_recv()
            total = total + part2_recv[d, :, cols].astype(jnp.float32)
        for b in range(4):
            fold[b, :seqs, cols] = total[b * seqs : (b + 1) * seqs, :]
        for d in (2, 1, 3):
            sum_z(h, d).start()
    for h in range(2):
        cols = slice(h * span, (h + 1) * span)
        total = fold[zh, :, cols]
        for d in (1, 3, 2):
            sum_z(h, d).wait_recv()
            total = total + fold_recv[d, :, cols]
        out_ref[:, cols] = total[:seqs, :]

    @pl.when(native)
    def _():
        for m in range(2):
            for s in range(2):
                z_copy(m, s, place(zl, y, m, beside, x), 1, m).wait_send()

                @pl.when(core != m)
                def _():
                    z_copy(m, s, sibling, 0, 2).wait_send()

        pin_remote.wait_send()

        @pl.when(next_to_across)
        def _():
            for s in range(4):
                quarter_out(s).wait_send()

    @pl.when(foreign)
    def _():
        for s in range(2):
            for m in range(2):
                z_copy(m, s, place(zl, y, m, across, x), 2, m).wait_send()
        for s in range(4):

            @pl.when(next_to_across)
            def _():
                quarter_on(s).wait_send()

            quarter_up(s).wait_send()
            quarter_down(s).wait_send()
            far_quarter(s).wait_send()
        left_copy(0).wait_send()

    for s in range(2):
        z_forward(s).wait_send()
    for j in range(4):
        for k in range(6):
            x_copy(j, k).wait_send()
        for k in range(4):
            sib_copy(j, k).wait_send()

    def left_done(d, carry):
        left_copy(d).wait_send()
        return carry

    lax.fori_loop(1, N, left_done, 0)
    for d in range(1, 4):
        grads_z(d).wait_send()
        for h in range(2):
            sum_x(h, d).wait_send()
            sum_z(h, d).wait_send()
    for d in range(4):
        for e in range(1, 4):
            grads_x(d, e).wait_send()
    for sent in (right_sent, rall_sent, part_sent, pall_sent):
        sent()


def body(inputs, cotangent, gate_weight, up_weight, proj_in, proj_out, inverse_fisher, stored):
    tokens, width = inputs.shape
    units = gate_weight.shape[1]
    feats, wide = inverse_fisher.shape
    rows = N * (tokens // TOK_SEQ)
    f32, bf16 = jnp.float32, jnp.bfloat16
    dma = pltpu.SemaphoreType.DMA
    return pl.pallas_call(
        scores_kernel,
        out_shape=jax.ShapeDtypeStruct((tokens // TOK_SEQ, stored.shape[0]), f32),
        in_specs=[pl.BlockSpec(memory_space=pl.ANY)] * 8,
        out_specs=pl.BlockSpec(memory_space=pltpu.VMEM),
        scratch_shapes=[
            pltpu.VMEM((2, width, units), bf16),
            pltpu.VMEM((tokens, width), bf16),
            pltpu.VMEM((tokens, units), f32),
            pltpu.VMEM((tokens, units), f32),
            pltpu.VMEM((units, KIN), bf16),
            pltpu.VMEM(cotangent.shape, bf16),
            pltpu.VMEM(proj_out.shape, bf16),
            pltpu.VMEM(inverse_fisher.shape, bf16),
            pltpu.VMEM(stored.shape, bf16),
            pltpu.VMEM((KIN, tokens), f32),
            pltpu.VMEM((N, 8, tokens), f32),
            pltpu.VMEM((tokens, KOUT), f32),
            pltpu.VMEM((N, tokens // N, KOUT), f32),
            pltpu.VMEM((tokens // N, KOUT), f32),
            pltpu.VMEM((tokens, KOUT), f32),
            pltpu.VMEM((N * PAD, feats), bf16),
            pltpu.VMEM((rows, wide), f32),
            pltpu.VMEM((rows, wide), bf16),
            pltpu.VMEM((N, rows // 4, wide // 4), bf16),
            pltpu.VMEM((rows // 4, wide // 4), bf16),
            pltpu.VMEM((rows, wide), bf16),
            pltpu.VMEM((rows, stored.shape[0]), bf16),
            pltpu.VMEM((4, rows // 4, stored.shape[0]), bf16),
            pltpu.VMEM((4, PAD, stored.shape[0]), f32),
            pltpu.VMEM((4, PAD, stored.shape[0]), f32),
            dma((7,)),
            dma((4, 2)), dma((4, 2)),
            dma((4, 6)), dma((4, 6)),
            dma((4, 4)), dma((4, 4)),
            dma((21,)), dma((21,)),
            dma((8, N)), dma((8, N)),
        ],
        compiler_params=pltpu.CompilerParams(
            collective_id=1, has_side_effects=True, vmem_limit_bytes=60 * 1024 * 1024),
        name="scores",
    )(inputs, cotangent, gate_weight, up_weight, proj_in, proj_out, inverse_fisher, stored)


def solution(mesh):
    return jax.shard_map(
        body,
        mesh=mesh,
        in_specs=(
            P("col", None),
            P("col", "row"),
            P("col", "row"),
            P("col", "row"),
            P("row", None),
            P("row", None),
            P("row", "col"),
            P("row", "col"),
        ),
        out_specs=P("col", "row"),
        check_vma=False,
    )
```

```python
import jax
import jax.numpy as jnp
from jax import lax
from jax.experimental import pallas as pl
from jax.experimental.pallas import tpu as pltpu
from jax.sharding import PartitionSpec as P

KIN = 128
KOUT = 128
TOK_SEQ = 64
N = 16
PAD = 16
TILE = 256


def place(zl, y, core, zh, x):
    return {"row": (zl * 4 + y) * 2 + core, "col": zh * 4 + x}


def remote(src, dst, send, recv, device):
    return pltpu.make_async_remote_copy(
        src_ref=src, dst_ref=dst, send_sem=send, recv_sem=recv, device_id=device)


def scores_kernel(
    x_hbm, cot_hbm, gate_hbm, up_hbm, pin_hbm, pout_hbm, fisher_hbm, stored_hbm, out_ref,
    weights, acts, acc_gate, acc_up, pin, cot, pout, fisher, stored,
    left_part, left_recv, right_part, right_recv, right_own, right_all,
    grads_all, packed, part, part_recv, prec_own, prec_all, part2, part2_recv, fold, fold_recv,
    local_sem, z_send, z_recv, x_send, x_recv, sib_send, sib_recv, in_send, in_recv,
    tail_send, tail_recv,
):
    row = lax.axis_index("row")
    col = lax.axis_index("col")
    core = lax.rem(row, 2)
    y = lax.rem(row // 2, 4)
    zl = row // 8
    x = lax.rem(col, 4)
    zh = col // 4
    kind = zh // 2
    native = core == kind
    foreign = core != kind
    beside = zh + 1 - 2 * lax.rem(zh, 2)
    across = 3 - zh
    across_beside = across + 1 - 2 * lax.rem(across, 2)
    next_to_across = lax.rem(zh, 2) == zl
    sources = (zh, beside, across, across_beside)
    right = lax.rem(x + 1, 4)
    left = lax.rem(x + 3, 4)
    far = lax.rem(x + 2, 4)
    sides = (x, left, right, far)
    up_y = lax.rem(y + 1, 4)
    down_y = lax.rem(y + 3, 4)
    depth = gate_hbm.shape[0]
    sub = depth // 2
    group = 4 * depth
    tokens = x_hbm.shape[0]
    quarter = tokens // 4
    slab = quarter // 4
    tok_blk = tokens // N
    seqs = tokens // TOK_SEQ
    high = 4 * seqs
    broad = fisher.shape[1] // 4
    sibling = place(zl, y, 1 - core, zh, x)
    token_col = jnp.where(native, zh, across) * 4 + x

    def row_dev(d):
        return {"row": lax.rem(row + d, N), "col": col}

    loads = [
        pltpu.make_async_copy(a, b, local_sem.at[i])
        for i, (a, b) in enumerate(
            [(cot_hbm, cot), (pout_hbm, pout), (fisher_hbm, fisher), (stored_hbm, stored)])
    ]
    acts_copy = pltpu.make_async_copy(x_hbm, acts, local_sem.at[4])
    pin_copy = pltpu.make_async_copy(pin_hbm, pin, local_sem.at[5])
    for load in loads:
        load.start()

    fold[...] = jnp.zeros_like(fold)
    barrier = pltpu.get_barrier_semaphore()
    partners = [{"row": lax.rem(row + d, N), "col": across * 4 + x} for d in range(N)]
    partners += [place(zl, y, core, across_beside, x)]
    partners += [place(zl, y, core, zh, side) for side in (far, right, left)]
    partners += [place(zl, y, 0, beside, x), place(zl, y, 1, beside, x)]
    partners += [row_dev(d) for d in range(1, N)]
    for partner in partners:
        pl.semaphore_signal(barrier, inc=1, device_id=partner)
    pl.semaphore_wait(barrier, len(partners))

    def block(m, zs, xs, start=0, rows=depth):
        return weights.at[m, pl.ds(zs * group + xs * depth + start, rows)]

    mats = (gate_hbm, up_hbm)

    def z_copy(m, s, device, j, slot):
        return remote(mats[m].at[pl.ds(s * sub, sub)], block(m, zh, x, s * sub, sub),
                      z_send.at[slot, s], z_recv.at[j, s], device)

    def z_forward(s):
        ref = block(core, across, x, s * sub, sub)
        return remote(ref, ref, z_send.at[3, s], z_recv.at[3, s], place(zl, y, core, beside, x))

    def z_arrival(j, s):
        ref = block(core, sources[j], x, s * sub, sub)
        return remote(ref, ref, z_send.at[3, s], z_recv.at[j, s], sibling)

    def in_copy(src_ref, q, s, slot, recv_slot, device):
        at = pl.ds(q * quarter + s * slab, slab)
        return remote(src_ref.at[at], acts.at[at], in_send.at[slot], in_recv.at[recv_slot], device)

    pin_remote = remote(pin_hbm, pin, in_send.at[0], in_recv.at[0], sibling)

    def quarter_out(s):
        return in_copy(x_hbm, y, s, 1 + s, 1 + s, place(1 - zl, y, core, across, x))

    def quarter_on(s):
        return in_copy(acts, y, s, 5 + s, 1 + s, place(1 - zl, y, core, zh, x))

    def quarter_up(s):
        return in_copy(acts, y, s, 9 + s, 9 + s, place(zl, up_y, core, zh, x))

    def quarter_down(s):
        return in_copy(acts, y, s, 13 + s, 13 + s, place(zl, down_y, core, zh, x))

    def far_quarter(s):
        if s < 2:
            return in_copy(acts, down_y, s, 17 + s, 17 + s, place(zl, up_y, core, zh, x))
        return in_copy(acts, up_y, s, 17 + s, 17 + s, place(zl, down_y, core, zh, x))

    def own_copy(m):
        return pltpu.make_async_copy(mats[m], block(m, zh, x), local_sem.at[6])

    @pl.when(native)
    def _():
        for m in range(2):

            @pl.when(core == m)
            def _():
                own_copy(m).start()

            @pl.when(core != m)
            def _():
                for s in range(2):
                    z_copy(m, s, sibling, 0, 2).start()

        @pl.when(next_to_across)
        def _():
            for s in range(4):
                quarter_out(s).start()

        for s in range(2):
            for m in range(2):
                z_copy(m, s, place(zl, y, m, beside, x), 1, m).start()
        for m in range(2):

            @pl.when(core == m)
            def _():
                own_copy(m).wait()

        pin_remote.start()
        pin_copy.start()
        acts_copy.start()

    def across_start(s):
        @pl.when(foreign)
        def _():
            for m in range(2):
                z_copy(m, s, place(zl, y, m, across, x), 2, m).start()

    def sib_copy(j, k):
        ref = block(core, sources[j], sides[k])
        return remote(ref, ref, sib_send.at[j, k], sib_recv.at[j, k], sibling)

    def x_copy(j, k):
        side, s = (k // 2, k % 2) if k < 4 else (k - 4, k - 4)
        whose = x if k < 4 else (left, right)[side]
        ref = block(core, sources[j], whose, s * sub, sub)
        return remote(ref, ref, x_send.at[j, k], x_recv.at[j, k],
                      place(zl, y, core, zh, (right, left)[side]))

    def have_column(j, s):
        if j > 0:
            z_arrival(j, s).wait_recv()
        else:

            @pl.when(foreign)
            def _():
                z_arrival(0, s).wait_recv()

        if j == 2:
            z_forward(s).start()
        x_copy(j, s).start()
        x_copy(j, 2 + s).start()
        if s == 1:
            sib_copy(j, 0).start()

    def have_side(j, s):
        for side in range(2):
            x_copy(j, 2 * side + s).wait_recv()
            if s == side:
                x_copy(j, 4 + s).start()
            if s == 1:
                sib_copy(j, 1 + side).start()

    def have_far(j):
        x_copy(j, 4).wait_recv()
        x_copy(j, 5).wait_recv()
        sib_copy(j, 3).start()

    def sib_arrival(j, k):
        ref = block(1 - core, sources[j], sides[k])
        remote(ref, ref, sib_send.at[j, k], sib_recv.at[j, k], sibling).wait_recv()

    def have_quarter(s):
        @pl.when(foreign)
        def _():
            quarter_out(s).wait_recv()

            @pl.when(next_to_across)
            def _():
                quarter_on(s).start()

            quarter_up(s).start()
            quarter_down(s).start()

    def pass_quarter(s):
        @pl.when(foreign)
        def _():
            quarter_up(s).wait_recv()
            quarter_down(s).wait_recv()
            far_quarter(s).start()

    def have_inputs():
        @pl.when(foreign)
        def _():
            for s in range(4):
                far_quarter(s).wait_recv()
            pin_remote.wait_recv()

        @pl.when(native)
        def _():
            pin_copy.wait()

    def own_kind():
        @pl.when(native)
        def _():
            acts_copy.wait()

    def many(phase, src_of, dst_of, dev_of, first=1, last=N):
        def copy(d):
            return remote(src_of(d), dst_of(d), tail_send.at[phase, d], tail_recv.at[phase, d], dev_of(d))

        def run(action):
            def step(d, carry):
                action(copy(d))
                return carry

            lax.fori_loop(first, last, step, 0)

        run(lambda c: c.start())
        return lambda: run(lambda c: c.wait_recv()), lambda: run(lambda c: c.wait_send())

    def at_row(d):
        return lax.rem(row + d, N)

    def deep_dot(rows, start, size):
        deep = pl.ds(pl.multiple_of(start, 256), size)
        a = acts[rows, deep]
        return (jnp.dot(a, weights[0, deep, :], preferred_element_type=jnp.float32),
                jnp.dot(a, weights[1, deep, :], preferred_element_type=jnp.float32))

    def group_dot(j, rows):
        return deep_dot(rows, sources[j] * group, group)

    def piece_dot(j, k, rows):
        return deep_dot(rows, sources[j] * group + sides[k] * depth, depth)

    def tiles(step):
        def at(t, carry):
            step(pl.ds(pl.multiple_of(t * TILE, TILE), TILE))
            return carry

        lax.fori_loop(0, tokens // TILE, at, 0)

    def quarter_rows(ahead):
        return pl.ds(pl.multiple_of(lax.rem(y + ahead, 4) * quarter, 64), quarter)

    def compute_near(j):
        def step(t, carry):
            rows = quarter_rows(t + t // 2)
            gate, up = group_dot(j, rows)
            if j == 0:
                acc_gate[rows, :] = gate
                acc_up[rows, :] = up
            else:
                acc_gate[rows, :] += gate
                acc_up[rows, :] += up
            return carry

        lax.fori_loop(0, 3, step, 0)

    def compute_last():
        rows = quarter_rows(2)
        gate0, up0 = group_dot(0, rows)
        gate1, up1 = group_dot(1, rows)
        acc_gate[rows, :] = gate0 + gate1
        acc_up[rows, :] = up0 + up1

    def compute_add(j):
        def step(rows):
            gate, up = group_dot(j, rows)
            acc_gate[rows, :] += gate
            acc_up[rows, :] += up

        tiles(step)

    def compute_pieces(j):
        def step(rows):
            for m, acc in ((0, acc_gate), (1, acc_up)):
                total = acc[rows, :]
                for k in range(3):
                    deep = pl.ds(pl.multiple_of(sources[j] * group + sides[k] * depth, 256), depth)
                    total = total + jnp.dot(acts[rows, deep], weights[m, deep, :], preferred_element_type=jnp.float32)
                acc[rows, :] = total

        tiles(step)

    def sibs(j, first=0, last=4):
        for k in range(first, last):
            sib_arrival(j, k)

    have_column(0, 0)
    have_column(0, 1)
    loads[0].wait()
    loads[1].wait()
    right_part[...] = jnp.dot(cot[...], pout[...], preferred_element_type=jnp.float32)
    right_in, right_sent = many(
        0, lambda d: right_part.at[pl.ds(at_row(d) * tok_blk, tok_blk)],
        lambda d: right_recv.at[d], row_dev)
    have_side(0, 0)
    across_start(0)
    have_quarter(0)
    have_side(0, 1)
    across_start(1)
    have_column(1, 0)
    have_quarter(1)
    have_far(0)
    have_column(1, 1)
    have_quarter(2)
    pass_quarter(0)
    have_column(2, 0)
    have_side(1, 0)
    have_quarter(3)
    pass_quarter(1)
    have_side(1, 1)
    have_column(2, 1)
    right_in()
    total = right_part[pl.ds(row * tok_blk, tok_blk), :]
    for d in range(1, N):
        total = total + right_recv[d]
    right_own[...] = total
    right_all[pl.ds(row * tok_blk, tok_blk), :] = total
    rall_in, rall_sent = many(
        2, lambda d: right_own,
        lambda d: right_all.at[pl.ds(row * tok_blk, tok_blk)], row_dev)

    pass_quarter(2)
    have_far(1)
    have_column(3, 0)
    pass_quarter(3)
    have_side(2, 0)
    have_column(3, 1)
    have_side(2, 1)
    own_kind()
    sibs(0)
    compute_near(0)
    have_side(3, 0)
    sibs(1)
    compute_near(1)
    have_side(3, 1)
    have_far(2)
    have_inputs()
    compute_last()
    sibs(2)
    compute_add(2)
    sibs(3, 0, 3)
    compute_pieces(3)
    have_far(3)
    sibs(3, 3, 4)

    def finish(rows):
        gate, up = piece_dot(3, 3, rows)
        gate = acc_gate[rows, :] + gate
        up = acc_up[rows, :] + up
        hidden = (gate / (1.0 + jnp.exp(-gate)) * up).astype(jnp.bfloat16)
        left_part[:, rows] = lax.dot_general(
            pin[...], hidden, (((0,), (1,)), ((), ())), preferred_element_type=jnp.float32)

    tiles(finish)

    slot = row - core + jnp.where(native, 0, 1)

    def left_copy(d):
        to = at_row(d)
        return remote(left_part.at[pl.ds(to * 8, 8)], left_recv.at[slot],
                      tail_send.at[1, d], tail_recv.at[1, slot], {"row": to, "col": token_col})

    def left_start(d, carry):
        left_copy(d).start()
        return carry

    lax.fori_loop(1, N, left_start, 0)

    @pl.when(native)
    def _():
        left_recv[pl.ds(slot, 1)] = left_part[pl.ds(row * 8, 8), :][None]

    @pl.when(foreign)
    def _():
        left_copy(0).start()

    rall_in()

    def left_wait(s, carry):
        @pl.when(foreign | (s != slot))
        def _():
            remote(left_recv.at[s], left_recv.at[s], tail_send.at[1, 0], tail_recv.at[1, s], sibling).wait_recv()

        return carry

    lax.fori_loop(0, N, left_wait, 0)
    total = left_recv[0]
    for d in range(1, N):
        total = total + left_recv[d]
    lane = lax.broadcasted_iota(jnp.int32, (PAD, tokens), 1)
    first = lax.broadcasted_iota(jnp.int32, (PAD, tokens), 0) * TOK_SEQ
    inside = (lane >= first) & (lane < first + TOK_SEQ)
    spread = jnp.concatenate(
        [jnp.where(inside, jnp.broadcast_to(total[i : i + 1, :], (PAD, tokens)), 0.0) for i in range(8)], axis=0)
    grads = jnp.dot(spread, right_all[...], preferred_element_type=jnp.float32, precision=lax.Precision.HIGHEST)
    mine = pl.ds(pl.multiple_of((x * 4 + zh) * PAD, PAD), PAD)
    for i in range(8):
        grads_all[mine, i * KOUT : (i + 1) * KOUT] = grads[i * PAD : (i + 1) * PAD, :].astype(jnp.bfloat16)

    def z_dev(d):
        return place(zl, y, core, lax.rem(zh + d, 4), x)

    def x_dev(d):
        return place(zl, y, core, zh, lax.rem(x + d, 4))

    def grads_z(d):
        return remote(grads_all.at[mine], grads_all.at[mine], tail_send.at[3, d], tail_recv.at[3, d], z_dev(d))

    def grads_x(d, e):
        at = grads_all.at[pl.ds((x * 4 + lax.rem(zh + 4 - d, 4)) * PAD, PAD)]
        return remote(at, at, tail_send.at[7, d * 3 + e - 1], tail_recv.at[7, d * 3 + e - 1], x_dev(e))

    for d in (2, 1, 3):
        grads_z(d).start()
    for d in (0, 1, 3, 2):
        if d > 0:
            grads_z(d).wait_recv()
        for e in (2, 1, 3):
            grads_x(d, e).start()
    loads[2].wait()
    for d in (0, 1, 3, 2):
        for e in (1, 3, 2):
            grads_x(d, e).wait_recv()
    padded = jnp.dot(grads_all[...], fisher[...], preferred_element_type=jnp.float32)
    for b in range(N):
        packed[b * seqs : (b + 1) * seqs, :] = padded[b * PAD : b * PAD + seqs, :]
    part[...] = packed[...].astype(jnp.bfloat16)

    def piece(r):
        return (pl.ds(pl.multiple_of(r // 4 * high, high), high), pl.ds(pl.multiple_of(lax.rem(r, 4) * broad, broad), broad))

    part_in, part_sent = many(4, lambda d: part.at[piece(at_row(d))], lambda d: part_recv.at[d], row_dev)
    part_in()
    total = part[piece(row)].astype(jnp.float32)
    for d in range(1, N):
        total = total + part_recv[d].astype(jnp.float32)
    prec_own[...] = total.astype(jnp.bfloat16)
    prec_all[piece(row)] = total.astype(jnp.bfloat16)
    pall_in, pall_sent = many(5, lambda d: prec_own, lambda d: prec_all.at[piece(row)], row_dev)
    loads[3].wait()
    pall_in()
    span = stored.shape[0] // 2
    column = pl.ds(pl.multiple_of(x * high, high), high)

    def sum_x(h, d):
        return remote(
            part2.at[pl.ds(lax.rem(x + d, 4) * high, high), pl.ds(h * span, span)],
            part2_recv.at[d, :, pl.ds(h * span, span)],
            tail_send.at[6, h * 8 + d], tail_recv.at[6, h * 8 + d], x_dev(d))

    def sum_z(h, d):
        return remote(
            fold.at[lax.rem(zh + d, 4), :, pl.ds(h * span, span)],
            fold_recv.at[d, :, pl.ds(h * span, span)],
            tail_send.at[6, h * 8 + 4 + d], tail_recv.at[6, h * 8 + 4 + d], z_dev(d))

    for h in range(2):
        cols = slice(h * span, (h + 1) * span)
        part2[:, cols] = lax.dot_general(
            prec_all[...], stored[cols, :], (((1,), (1,)), ((), ())),
            preferred_element_type=jnp.float32).astype(jnp.bfloat16)
        for d in (2, 1, 3):
            sum_x(h, d).start()
    for h in range(2):
        cols = slice(h * span, (h + 1) * span)
        total = part2[column, cols].astype(jnp.float32)
        for d in (1, 3, 2):
            sum_x(h, d).wait_recv()
            total = total + part2_recv[d, :, cols].astype(jnp.float32)
        for b in range(4):
            fold[b, :seqs, cols] = total[b * seqs : (b + 1) * seqs, :]
        for d in (2, 1, 3):
            sum_z(h, d).start()
    for h in range(2):
        cols = slice(h * span, (h + 1) * span)
        total = fold[zh, :, cols]
        for d in (1, 3, 2):
            sum_z(h, d).wait_recv()
            total = total + fold_recv[d, :, cols]
        out_ref[:, cols] = total[:seqs, :]

    @pl.when(native)
    def _():
        for m in range(2):
            for s in range(2):
                z_copy(m, s, place(zl, y, m, beside, x), 1, m).wait_send()

                @pl.when(core != m)
                def _():
                    z_copy(m, s, sibling, 0, 2).wait_send()

        pin_remote.wait_send()

        @pl.when(next_to_across)
        def _():
            for s in range(4):
                quarter_out(s).wait_send()

    @pl.when(foreign)
    def _():
        for s in range(2):
            for m in range(2):
                z_copy(m, s, place(zl, y, m, across, x), 2, m).wait_send()
        for s in range(4):

            @pl.when(next_to_across)
            def _():
                quarter_on(s).wait_send()

            quarter_up(s).wait_send()
            quarter_down(s).wait_send()
            far_quarter(s).wait_send()
        left_copy(0).wait_send()

    for s in range(2):
        z_forward(s).wait_send()
    for j in range(4):
        for k in range(6):
            x_copy(j, k).wait_send()
        for k in range(4):
            sib_copy(j, k).wait_send()

    def left_done(d, carry):
        left_copy(d).wait_send()
        return carry

    lax.fori_loop(1, N, left_done, 0)
    for d in range(1, 4):
        grads_z(d).wait_send()
        for h in range(2):
            sum_x(h, d).wait_send()
            sum_z(h, d).wait_send()
    for d in range(4):
        for e in range(1, 4):
            grads_x(d, e).wait_send()
    for sent in (right_sent, rall_sent, part_sent, pall_sent):
        sent()


def body(inputs, cotangent, gate_weight, up_weight, proj_in, proj_out, inverse_fisher, stored):
    tokens, width = inputs.shape
    units = gate_weight.shape[1]
    feats, wide = inverse_fisher.shape
    rows = N * (tokens // TOK_SEQ)
    f32, bf16 = jnp.float32, jnp.bfloat16
    dma = pltpu.SemaphoreType.DMA
    return pl.pallas_call(
        scores_kernel,
        out_shape=jax.ShapeDtypeStruct((tokens // TOK_SEQ, stored.shape[0]), f32),
        in_specs=[pl.BlockSpec(memory_space=pl.ANY)] * 8,
        out_specs=pl.BlockSpec(memory_space=pltpu.VMEM),
        scratch_shapes=[
            pltpu.VMEM((2, width, units), bf16),
            pltpu.VMEM((tokens, width), bf16),
            pltpu.VMEM((tokens, units), f32),
            pltpu.VMEM((tokens, units), f32),
            pltpu.VMEM((units, KIN), bf16),
            pltpu.VMEM(cotangent.shape, bf16),
            pltpu.VMEM(proj_out.shape, bf16),
            pltpu.VMEM(inverse_fisher.shape, bf16),
            pltpu.VMEM(stored.shape, bf16),
            pltpu.VMEM((KIN, tokens), f32),
            pltpu.VMEM((N, 8, tokens), f32),
            pltpu.VMEM((tokens, KOUT), f32),
            pltpu.VMEM((N, tokens // N, KOUT), f32),
            pltpu.VMEM((tokens // N, KOUT), f32),
            pltpu.VMEM((tokens, KOUT), f32),
            pltpu.VMEM((N * PAD, feats), bf16),
            pltpu.VMEM((rows, wide), f32),
            pltpu.VMEM((rows, wide), bf16),
            pltpu.VMEM((N, rows // 4, wide // 4), bf16),
            pltpu.VMEM((rows // 4, wide // 4), bf16),
            pltpu.VMEM((rows, wide), bf16),
            pltpu.VMEM((rows, stored.shape[0]), bf16),
            pltpu.VMEM((4, rows // 4, stored.shape[0]), bf16),
            pltpu.VMEM((4, PAD, stored.shape[0]), f32),
            pltpu.VMEM((4, PAD, stored.shape[0]), f32),
            dma((7,)),
            dma((4, 2)), dma((4, 2)),
            dma((4, 6)), dma((4, 6)),
            dma((4, 4)), dma((4, 4)),
            dma((21,)), dma((21,)),
            dma((8, N)), dma((8, N)),
        ],
        compiler_params=pltpu.CompilerParams(
            collective_id=1, has_side_effects=True, vmem_limit_bytes=60 * 1024 * 1024),
        name="scores",
    )(inputs, cotangent, gate_weight, up_weight, proj_in, proj_out, inverse_fisher, stored)


def solution(mesh):
    return jax.shard_map(
        body,
        mesh=mesh,
        in_specs=(
            P("col", None),
            P("col", "row"),
            P("col", "row"),
            P("col", "row"),
            P("row", None),
            P("row", None),
            P("row", "col"),
            P("row", "col"),
        ),
        out_specs=P("col", "row"),
        check_vma=False,
    )
```

```python
import jax
import jax.numpy as jnp
from jax import lax
from jax.experimental import pallas as pl
from jax.experimental.pallas import tpu as pltpu
from jax.sharding import PartitionSpec as P

KIN = 128
KOUT = 128
TOK_SEQ = 64
N = 16
PAD = 16
TILE = 384


def place(zl, y, core, zh, x):
    return {"row": (zl * 4 + y) * 2 + core, "col": zh * 4 + x}


def remote(src, dst, send, recv, device):
    return pltpu.make_async_remote_copy(
        src_ref=src, dst_ref=dst, send_sem=send, recv_sem=recv, device_id=device)


def scores_kernel(
    x_hbm, cot_hbm, gate_hbm, up_hbm, pin_hbm, pout_hbm, fisher_hbm, stored_hbm, out_ref,
    weights, acts, acc_gate, acc_up, pin, cot, pout, fisher, stored,
    left_part, left_recv, right_part, right_recv, right_own, right_all,
    grads_all, packed, part, part_recv, prec_own, prec_all, part2, part2_recv, fold, fold_recv,
    local_sem, z_send, z_recv, x_send, x_recv, sib_send, sib_recv, in_send, in_recv,
    tail_send, tail_recv,
):
    row = lax.axis_index("row")
    col = lax.axis_index("col")
    core = lax.rem(row, 2)
    y = lax.rem(row // 2, 4)
    zl = row // 8
    x = lax.rem(col, 4)
    zh = col // 4
    kind = zh // 2
    native = core == kind
    foreign = core != kind
    beside = zh + 1 - 2 * lax.rem(zh, 2)
    across = 3 - zh
    across_beside = across + 1 - 2 * lax.rem(across, 2)
    next_to_across = lax.rem(zh, 2) == zl
    sources = (zh, beside, across, across_beside)
    right = lax.rem(x + 1, 4)
    left = lax.rem(x + 3, 4)
    far = lax.rem(x + 2, 4)
    sides = (x, left, right, far)
    up_y = lax.rem(y + 1, 4)
    down_y = lax.rem(y + 3, 4)
    depth = gate_hbm.shape[0]
    sub = depth // 2
    group = 4 * depth
    tokens = x_hbm.shape[0]
    quarter = tokens // 4
    slab = quarter // 4
    tok_blk = tokens // N
    seqs = tokens // TOK_SEQ
    high = 4 * seqs
    broad = fisher.shape[1] // 4
    sibling = place(zl, y, 1 - core, zh, x)
    token_col = jnp.where(native, zh, across) * 4 + x

    def row_dev(d):
        return {"row": lax.rem(row + d, N), "col": col}

    loads = [
        pltpu.make_async_copy(a, b, local_sem.at[i])
        for i, (a, b) in enumerate(
            [(cot_hbm, cot), (pout_hbm, pout), (fisher_hbm, fisher), (stored_hbm, stored)])
    ]
    acts_copy = pltpu.make_async_copy(x_hbm, acts, local_sem.at[4])
    pin_copy = pltpu.make_async_copy(pin_hbm, pin, local_sem.at[5])
    for load in loads:
        load.start()

    fold[...] = jnp.zeros_like(fold)
    barrier = pltpu.get_barrier_semaphore()
    partners = [{"row": lax.rem(row + d, N), "col": across * 4 + x} for d in range(N)]
    partners += [place(zl, y, core, across_beside, x)]
    partners += [place(zl, y, core, zh, side) for side in (far, right, left)]
    partners += [place(zl, y, 0, beside, x), place(zl, y, 1, beside, x)]
    partners += [row_dev(d) for d in range(1, N)]
    for partner in partners:
        pl.semaphore_signal(barrier, inc=1, device_id=partner)
    pl.semaphore_wait(barrier, len(partners))

    def block(m, zs, xs, start=0, rows=depth):
        return weights.at[m, pl.ds(zs * group + xs * depth + start, rows)]

    mats = (gate_hbm, up_hbm)

    def z_copy(m, s, device, j, slot):
        return remote(mats[m].at[pl.ds(s * sub, sub)], block(m, zh, x, s * sub, sub),
                      z_send.at[slot, s], z_recv.at[j, s], device)

    def z_forward(s):
        ref = block(core, across, x, s * sub, sub)
        return remote(ref, ref, z_send.at[3, s], z_recv.at[3, s], place(zl, y, core, beside, x))

    def z_arrival(j, s):
        ref = block(core, sources[j], x, s * sub, sub)
        return remote(ref, ref, z_send.at[3, s], z_recv.at[j, s], sibling)

    def in_copy(src_ref, q, s, slot, recv_slot, device):
        at = pl.ds(q * quarter + s * slab, slab)
        return remote(src_ref.at[at], acts.at[at], in_send.at[slot], in_recv.at[recv_slot], device)

    pin_remote = remote(pin_hbm, pin, in_send.at[0], in_recv.at[0], sibling)

    def quarter_out(s):
        return in_copy(x_hbm, y, s, 1 + s, 1 + s, place(1 - zl, y, core, across, x))

    def quarter_on(s):
        return in_copy(acts, y, s, 5 + s, 1 + s, place(1 - zl, y, core, zh, x))

    def quarter_up(s):
        return in_copy(acts, y, s, 9 + s, 9 + s, place(zl, up_y, core, zh, x))

    def quarter_down(s):
        return in_copy(acts, y, s, 13 + s, 13 + s, place(zl, down_y, core, zh, x))

    def far_quarter(s):
        if s < 2:
            return in_copy(acts, down_y, s, 17 + s, 17 + s, place(zl, up_y, core, zh, x))
        return in_copy(acts, up_y, s, 17 + s, 17 + s, place(zl, down_y, core, zh, x))

    def own_copy(m):
        return pltpu.make_async_copy(mats[m], block(m, zh, x), local_sem.at[6])

    @pl.when(native)
    def _():
        for m in range(2):

            @pl.when(core == m)
            def _():
                own_copy(m).start()

            @pl.when(core != m)
            def _():
                for s in range(2):
                    z_copy(m, s, sibling, 0, 2).start()

        @pl.when(next_to_across)
        def _():
            for s in range(4):
                quarter_out(s).start()

        for s in range(2):
            for m in range(2):
                z_copy(m, s, place(zl, y, m, beside, x), 1, m).start()
        for m in range(2):

            @pl.when(core == m)
            def _():
                own_copy(m).wait()

        pin_remote.start()
        pin_copy.start()
        acts_copy.start()

    def across_start(s):
        @pl.when(foreign)
        def _():
            for m in range(2):
                z_copy(m, s, place(zl, y, m, across, x), 2, m).start()

    def sib_copy(j, k):
        ref = block(core, sources[j], sides[k])
        return remote(ref, ref, sib_send.at[j, k], sib_recv.at[j, k], sibling)

    def x_copy(j, k):
        side, s = (k // 2, k % 2) if k < 4 else (k - 4, k - 4)
        whose = x if k < 4 else (left, right)[side]
        ref = block(core, sources[j], whose, s * sub, sub)
        return remote(ref, ref, x_send.at[j, k], x_recv.at[j, k],
                      place(zl, y, core, zh, (right, left)[side]))

    def have_column(j, s):
        if j > 0:
            z_arrival(j, s).wait_recv()
        else:

            @pl.when(foreign)
            def _():
                z_arrival(0, s).wait_recv()

        if j == 2:
            z_forward(s).start()
        x_copy(j, s).start()
        x_copy(j, 2 + s).start()
        if s == 1:
            sib_copy(j, 0).start()

    def have_side(j, s):
        for side in range(2):
            x_copy(j, 2 * side + s).wait_recv()
            if s == side:
                x_copy(j, 4 + s).start()
            if s == 1:
                sib_copy(j, 1 + side).start()

    def have_far(j):
        x_copy(j, 4).wait_recv()
        x_copy(j, 5).wait_recv()
        sib_copy(j, 3).start()

    def sib_arrival(j, k):
        ref = block(1 - core, sources[j], sides[k])
        remote(ref, ref, sib_send.at[j, k], sib_recv.at[j, k], sibling).wait_recv()

    def have_quarter(s):
        @pl.when(foreign)
        def _():
            quarter_out(s).wait_recv()

            @pl.when(next_to_across)
            def _():
                quarter_on(s).start()

            quarter_up(s).start()
            quarter_down(s).start()

    def pass_quarter(s):
        @pl.when(foreign)
        def _():
            quarter_up(s).wait_recv()
            quarter_down(s).wait_recv()
            far_quarter(s).start()

    def have_inputs():
        @pl.when(foreign)
        def _():
            for s in range(4):
                far_quarter(s).wait_recv()
            pin_remote.wait_recv()

        @pl.when(native)
        def _():
            pin_copy.wait()

    def own_kind():
        @pl.when(native)
        def _():
            acts_copy.wait()

    def many(phase, src_of, dst_of, dev_of, first=1, last=N):
        def copy(d):
            return remote(src_of(d), dst_of(d), tail_send.at[phase, d], tail_recv.at[phase, d], dev_of(d))

        def run(action):
            def step(d, carry):
                action(copy(d))
                return carry

            lax.fori_loop(first, last, step, 0)

        run(lambda c: c.start())
        return lambda: run(lambda c: c.wait_recv()), lambda: run(lambda c: c.wait_send())

    def at_row(d):
        return lax.rem(row + d, N)

    def deep_dot(rows, start, size):
        deep = pl.ds(pl.multiple_of(start, 256), size)
        a = acts[rows, deep]
        return (jnp.dot(a, weights[0, deep, :], preferred_element_type=jnp.float32),
                jnp.dot(a, weights[1, deep, :], preferred_element_type=jnp.float32))

    def group_dot(j, rows):
        return deep_dot(rows, sources[j] * group, group)

    def piece_dot(j, k, rows):
        return deep_dot(rows, sources[j] * group + sides[k] * depth, depth)

    def tiles(step):
        def at(t, carry):
            step(pl.ds(pl.multiple_of(t * TILE, TILE), TILE))
            return carry

        lax.fori_loop(0, tokens // TILE, at, 0)

    def quarter_rows(ahead):
        return pl.ds(pl.multiple_of(lax.rem(y + ahead, 4) * quarter, 64), quarter)

    def compute_near(j):
        def step(t, carry):
            rows = quarter_rows(t + t // 2)
            gate, up = group_dot(j, rows)
            if j == 0:
                acc_gate[rows, :] = gate
                acc_up[rows, :] = up
            else:
                acc_gate[rows, :] += gate
                acc_up[rows, :] += up
            return carry

        lax.fori_loop(0, 3, step, 0)

    def compute_last():
        rows = quarter_rows(2)
        gate0, up0 = group_dot(0, rows)
        gate1, up1 = group_dot(1, rows)
        acc_gate[rows, :] = gate0 + gate1
        acc_up[rows, :] = up0 + up1

    def compute_add(j):
        def step(rows):
            gate, up = group_dot(j, rows)
            acc_gate[rows, :] += gate
            acc_up[rows, :] += up

        tiles(step)

    def compute_pieces(j):
        def step(rows):
            for m, acc in ((0, acc_gate), (1, acc_up)):
                total = acc[rows, :]
                for k in range(3):
                    deep = pl.ds(pl.multiple_of(sources[j] * group + sides[k] * depth, 256), depth)
                    total = total + jnp.dot(acts[rows, deep], weights[m, deep, :], preferred_element_type=jnp.float32)
                acc[rows, :] = total

        tiles(step)

    def sibs(j, first=0, last=4):
        for k in range(first, last):
            sib_arrival(j, k)

    have_column(0, 0)
    have_column(0, 1)
    loads[0].wait()
    loads[1].wait()
    right_part[...] = jnp.dot(cot[...], pout[...], preferred_element_type=jnp.float32)
    right_in, right_sent = many(
        0, lambda d: right_part.at[pl.ds(at_row(d) * tok_blk, tok_blk)],
        lambda d: right_recv.at[d], row_dev)
    have_side(0, 0)
    across_start(0)
    have_quarter(0)
    have_side(0, 1)
    across_start(1)
    have_column(1, 0)
    have_quarter(1)
    have_far(0)
    have_column(1, 1)
    have_quarter(2)
    pass_quarter(0)
    have_column(2, 0)
    have_side(1, 0)
    have_quarter(3)
    pass_quarter(1)
    have_side(1, 1)
    have_column(2, 1)
    right_in()
    total = right_part[pl.ds(row * tok_blk, tok_blk), :]
    for d in range(1, N):
        total = total + right_recv[d]
    right_own[...] = total
    right_all[pl.ds(row * tok_blk, tok_blk), :] = total
    rall_in, rall_sent = many(
        2, lambda d: right_own,
        lambda d: right_all.at[pl.ds(row * tok_blk, tok_blk)], row_dev)

    pass_quarter(2)
    have_far(1)
    have_column(3, 0)
    pass_quarter(3)
    have_side(2, 0)
    have_column(3, 1)
    have_side(2, 1)
    own_kind()
    sibs(0)
    compute_near(0)
    have_side(3, 0)
    sibs(1)
    compute_near(1)
    have_side(3, 1)
    have_far(2)
    have_inputs()
    compute_last()
    sibs(2)
    compute_add(2)
    sibs(3, 0, 3)
    compute_pieces(3)
    have_far(3)
    sibs(3, 3, 4)

    def finish(rows):
        gate, up = piece_dot(3, 3, rows)
        gate = acc_gate[rows, :] + gate
        up = acc_up[rows, :] + up
        hidden = (gate / (1.0 + jnp.exp(-gate)) * up).astype(jnp.bfloat16)
        left_part[:, rows] = lax.dot_general(
            pin[...], hidden, (((0,), (1,)), ((), ())), preferred_element_type=jnp.float32)

    tiles(finish)

    slot = row - core + jnp.where(native, 0, 1)

    def left_copy(d):
        to = at_row(d)
        return remote(left_part.at[pl.ds(to * 8, 8)], left_recv.at[slot],
                      tail_send.at[1, d], tail_recv.at[1, slot], {"row": to, "col": token_col})

    def left_start(d, carry):
        left_copy(d).start()
        return carry

    lax.fori_loop(1, N, left_start, 0)

    @pl.when(native)
    def _():
        left_recv[pl.ds(slot, 1)] = left_part[pl.ds(row * 8, 8), :][None]

    @pl.when(foreign)
    def _():
        left_copy(0).start()

    rall_in()

    def left_wait(s, carry):
        @pl.when(foreign | (s != slot))
        def _():
            remote(left_recv.at[s], left_recv.at[s], tail_send.at[1, 0], tail_recv.at[1, s], sibling).wait_recv()

        return carry

    lax.fori_loop(0, N, left_wait, 0)
    total = left_recv[0]
    for d in range(1, N):
        total = total + left_recv[d]
    lane = lax.broadcasted_iota(jnp.int32, (PAD, tokens), 1)
    first = lax.broadcasted_iota(jnp.int32, (PAD, tokens), 0) * TOK_SEQ
    inside = (lane >= first) & (lane < first + TOK_SEQ)
    spread = jnp.concatenate(
        [jnp.where(inside, jnp.broadcast_to(total[i : i + 1, :], (PAD, tokens)), 0.0) for i in range(8)], axis=0)
    grads = jnp.dot(spread, right_all[...], preferred_element_type=jnp.float32, precision=lax.Precision.HIGHEST)
    mine = pl.ds(pl.multiple_of((x * 4 + zh) * PAD, PAD), PAD)
    for i in range(8):
        grads_all[mine, i * KOUT : (i + 1) * KOUT] = grads[i * PAD : (i + 1) * PAD, :].astype(jnp.bfloat16)

    def z_dev(d):
        return place(zl, y, core, lax.rem(zh + d, 4), x)

    def x_dev(d):
        return place(zl, y, core, zh, lax.rem(x + d, 4))

    def grads_z(d):
        return remote(grads_all.at[mine], grads_all.at[mine], tail_send.at[3, d], tail_recv.at[3, d], z_dev(d))

    def grads_x(d, e):
        at = grads_all.at[pl.ds((x * 4 + lax.rem(zh + 4 - d, 4)) * PAD, PAD)]
        return remote(at, at, tail_send.at[7, d * 3 + e - 1], tail_recv.at[7, d * 3 + e - 1], x_dev(e))

    for d in (2, 1, 3):
        grads_z(d).start()
    for d in (0, 1, 3, 2):
        if d > 0:
            grads_z(d).wait_recv()
        for e in (2, 1, 3):
            grads_x(d, e).start()
    loads[2].wait()
    for d in (0, 1, 3, 2):
        for e in (1, 3, 2):
            grads_x(d, e).wait_recv()
    padded = jnp.dot(grads_all[...], fisher[...], preferred_element_type=jnp.float32)
    for b in range(N):
        packed[b * seqs : (b + 1) * seqs, :] = padded[b * PAD : b * PAD + seqs, :]
    part[...] = packed[...].astype(jnp.bfloat16)

    def piece(r):
        return (pl.ds(pl.multiple_of(r // 4 * high, high), high), pl.ds(pl.multiple_of(lax.rem(r, 4) * broad, broad), broad))

    part_in, part_sent = many(4, lambda d: part.at[piece(at_row(d))], lambda d: part_recv.at[d], row_dev)
    part_in()
    total = part[piece(row)].astype(jnp.float32)
    for d in range(1, N):
        total = total + part_recv[d].astype(jnp.float32)
    prec_own[...] = total.astype(jnp.bfloat16)
    prec_all[piece(row)] = total.astype(jnp.bfloat16)
    pall_in, pall_sent = many(5, lambda d: prec_own, lambda d: prec_all.at[piece(row)], row_dev)
    loads[3].wait()
    pall_in()
    span = stored.shape[0] // 2
    column = pl.ds(pl.multiple_of(x * high, high), high)

    def sum_x(h, d):
        return remote(
            part2.at[pl.ds(lax.rem(x + d, 4) * high, high), pl.ds(h * span, span)],
            part2_recv.at[d, :, pl.ds(h * span, span)],
            tail_send.at[6, h * 8 + d], tail_recv.at[6, h * 8 + d], x_dev(d))

    def sum_z(h, d):
        return remote(
            fold.at[lax.rem(zh + d, 4), :, pl.ds(h * span, span)],
            fold_recv.at[d, :, pl.ds(h * span, span)],
            tail_send.at[6, h * 8 + 4 + d], tail_recv.at[6, h * 8 + 4 + d], z_dev(d))

    for h in range(2):
        cols = slice(h * span, (h + 1) * span)
        part2[:, cols] = lax.dot_general(
            prec_all[...], stored[cols, :], (((1,), (1,)), ((), ())),
            preferred_element_type=jnp.float32).astype(jnp.bfloat16)
        for d in (2, 1, 3):
            sum_x(h, d).start()
    for h in range(2):
        cols = slice(h * span, (h + 1) * span)
        total = part2[column, cols].astype(jnp.float32)
        for d in (1, 3, 2):
            sum_x(h, d).wait_recv()
            total = total + part2_recv[d, :, cols].astype(jnp.float32)
        for b in range(4):
            fold[b, :seqs, cols] = total[b * seqs : (b + 1) * seqs, :]
        for d in (2, 1, 3):
            sum_z(h, d).start()
    for h in range(2):
        cols = slice(h * span, (h + 1) * span)
        total = fold[zh, :, cols]
        for d in (1, 3, 2):
            sum_z(h, d).wait_recv()
            total = total + fold_recv[d, :, cols]
        out_ref[:, cols] = total[:seqs, :]

    @pl.when(native)
    def _():
        for m in range(2):
            for s in range(2):
                z_copy(m, s, place(zl, y, m, beside, x), 1, m).wait_send()

                @pl.when(core != m)
                def _():
                    z_copy(m, s, sibling, 0, 2).wait_send()

        pin_remote.wait_send()

        @pl.when(next_to_across)
        def _():
            for s in range(4):
                quarter_out(s).wait_send()

    @pl.when(foreign)
    def _():
        for s in range(2):
            for m in range(2):
                z_copy(m, s, place(zl, y, m, across, x), 2, m).wait_send()
        for s in range(4):

            @pl.when(next_to_across)
            def _():
                quarter_on(s).wait_send()

            quarter_up(s).wait_send()
            quarter_down(s).wait_send()
            far_quarter(s).wait_send()
        left_copy(0).wait_send()

    for s in range(2):
        z_forward(s).wait_send()
    for j in range(4):
        for k in range(6):
            x_copy(j, k).wait_send()
        for k in range(4):
            sib_copy(j, k).wait_send()

    def left_done(d, carry):
        left_copy(d).wait_send()
        return carry

    lax.fori_loop(1, N, left_done, 0)
    for d in range(1, 4):
        grads_z(d).wait_send()
        for h in range(2):
            sum_x(h, d).wait_send()
            sum_z(h, d).wait_send()
    for d in range(4):
        for e in range(1, 4):
            grads_x(d, e).wait_send()
    for sent in (right_sent, rall_sent, part_sent, pall_sent):
        sent()


def body(inputs, cotangent, gate_weight, up_weight, proj_in, proj_out, inverse_fisher, stored):
    tokens, width = inputs.shape
    units = gate_weight.shape[1]
    feats, wide = inverse_fisher.shape
    rows = N * (tokens // TOK_SEQ)
    f32, bf16 = jnp.float32, jnp.bfloat16
    dma = pltpu.SemaphoreType.DMA
    return pl.pallas_call(
        scores_kernel,
        out_shape=jax.ShapeDtypeStruct((tokens // TOK_SEQ, stored.shape[0]), f32),
        in_specs=[pl.BlockSpec(memory_space=pl.ANY)] * 8,
        out_specs=pl.BlockSpec(memory_space=pltpu.VMEM),
        scratch_shapes=[
            pltpu.VMEM((2, width, units), bf16),
            pltpu.VMEM((tokens, width), bf16),
            pltpu.VMEM((tokens, units), f32),
            pltpu.VMEM((tokens, units), f32),
            pltpu.VMEM((units, KIN), bf16),
            pltpu.VMEM(cotangent.shape, bf16),
            pltpu.VMEM(proj_out.shape, bf16),
            pltpu.VMEM(inverse_fisher.shape, bf16),
            pltpu.VMEM(stored.shape, bf16),
            pltpu.VMEM((KIN, tokens), f32),
            pltpu.VMEM((N, 8, tokens), f32),
            pltpu.VMEM((tokens, KOUT), f32),
            pltpu.VMEM((N, tokens // N, KOUT), f32),
            pltpu.VMEM((tokens // N, KOUT), f32),
            pltpu.VMEM((tokens, KOUT), f32),
            pltpu.VMEM((N * PAD, feats), bf16),
            pltpu.VMEM((rows, wide), f32),
            pltpu.VMEM((rows, wide), bf16),
            pltpu.VMEM((N, rows // 4, wide // 4), bf16),
            pltpu.VMEM((rows // 4, wide // 4), bf16),
            pltpu.VMEM((rows, wide), bf16),
            pltpu.VMEM((rows, stored.shape[0]), bf16),
            pltpu.VMEM((4, rows // 4, stored.shape[0]), bf16),
            pltpu.VMEM((4, PAD, stored.shape[0]), f32),
            pltpu.VMEM((4, PAD, stored.shape[0]), f32),
            dma((7,)),
            dma((4, 2)), dma((4, 2)),
            dma((4, 6)), dma((4, 6)),
            dma((4, 4)), dma((4, 4)),
            dma((21,)), dma((21,)),
            dma((8, N)), dma((8, N)),
        ],
        compiler_params=pltpu.CompilerParams(
            collective_id=1, has_side_effects=True, vmem_limit_bytes=60 * 1024 * 1024),
        name="scores",
    )(inputs, cotangent, gate_weight, up_weight, proj_in, proj_out, inverse_fisher, stored)


def solution(mesh):
    return jax.shard_map(
        body,
        mesh=mesh,
        in_specs=(
            P("col", None),
            P("col", "row"),
            P("col", "row"),
            P("col", "row"),
            P("row", None),
            P("row", None),
            P("row", "col"),
            P("row", "col"),
        ),
        out_specs=P("col", "row"),
        check_vma=False,
    )
```
